32 devices in a mesh: rows: 16 (over z, y, core), rep: 2 (over x).
Axes of the slice: x: 2, y: 2, z: 4, core: 2. Of those that a mesh axis runs over, the one named last changes fastest.
Arguments:
- features: bfloat16 [16384, 256], P(('rows', 'rep')), may hold values from -6 to 6
- node_order: int32 [16384], P(('rows', 'rep')), may hold values from 0 to 16383, as said below
- layer_weight: bfloat16 [256, 256], replicated, may hold values from -0.375 to 0.375
- layer_bias: float32 [256], replicated, may hold values from -3 to 3
- tile_values: bfloat16 [3072, 128, 128], P(('rows', 'rep')), may hold values from 0.0009994507 to 0.049804688
- tile_coords: int32 [3072, 2], P(('rows', 'rep')), may hold values from 0 to 127, as said below
- tile_count: int32 [32], P(('rows', 'rep')), may hold values from 24 to 96, as said below
Outputs:
- mixed_out: bfloat16 [16384, 256], P(('rows', 'rep'))
The draws below stay inside these ranges and needn't reach their ends.
Inputs may be any that keep to these rules, and one draw needn't show every extreme that they name: `node_order`: each aligned block of 512 entries is a permutation of the positions of that block. `tile_coords`: with b = g // 2 and c = g % 2, every entry of group g names a tile row p with b * 8 <= p < (b + 1) * 8 and a tile column q with (q // 8) % 2 = c; no tile appears twice in a group. `tile_count`: in every block b the group with c = b % 2 is full.
All inputs are finite; a program needn't handle non-finite values.
Results may differ from the reference program's by a relative error of at most 0.014.
Values may be sent and summed in bfloat16 or wider, within the bound.
No kernel may reach another device: no remote copies, remote signals or barrier semaphores. Data moves between devices by JAX's collectives and lax.ppermute only.
A program may use at most 128 MiB of HBM per device.

```python
import math
import jax
import jax.numpy as jnp
from jax import lax

HID = 256
TILE = 128
ROW_DEV = 1024
TILE_ROWS = 8
SECTIONS = 8
SHARD = 512
TILE_CAP = 96
NODES = 16384
N_ROWS = 16
N_REP = 2


def tile_layout(key):
    base_key = jax.random.fold_in(key, 101)

    def one_device(device_index):
        device_key = jax.random.fold_in(base_key, device_index)
        block_index = device_index // N_REP
        replica = device_index % N_REP
        slot_ids = jax.random.permutation(jax.random.fold_in(device_key, 1), TILE_ROWS * SECTIONS * TILE_ROWS)[:TILE_CAP]
        tile_row = slot_ids // (SECTIONS * TILE_ROWS)
        remainder = slot_ids % (SECTIONS * TILE_ROWS)
        section_ids = remainder // TILE_ROWS
        within = remainder % TILE_ROWS
        global_row = block_index * TILE_ROWS + tile_row
        global_col = (section_ids * N_REP + replica) * TILE_ROWS + within
        light_count = jax.random.randint(jax.random.fold_in(device_key, 2), (), TILE_CAP // 4, TILE_CAP // 2 + 1)
        count_now = jnp.where(replica == block_index % N_REP, TILE_CAP, light_count)
        return (jnp.stack([global_row, global_col], axis=-1).astype(jnp.int32), count_now.astype(jnp.int32))
    coord_rows, count_rows = jax.vmap(one_device)(jnp.arange(N_ROWS * N_REP, dtype=jnp.int32))
    return (coord_rows.reshape(N_ROWS * N_REP * TILE_CAP, 2), count_rows)


def draw_tile_coords(key, part):
    return tile_layout(key)[0]


def draw_tile_count(key, part):
    return tile_layout(key)[1]


def draw_node_order(key, part):

    def one_block(block_index):
        shuffled = jax.random.permutation(jax.random.fold_in(key, block_index), SHARD)
        return (shuffled + block_index * SHARD).astype(jnp.int32)
    return jax.vmap(one_block)(jnp.arange(NODES // SHARD, dtype=jnp.int32)).reshape(NODES)


def levels(own_key, dims, split, least, high):
    factor_of = 1.0
    for dim, shards_of in split:
        draws = jax.random.uniform(jax.random.fold_in(jax.random.fold_in(own_key, 6), dim), (shards_of,), jnp.float32, least / len(split), high / len(split))
        factor_of = factor_of * jnp.repeat(jnp.exp(draws), dims[dim] // shards_of).reshape((-1,) + (1,) * (len(dims) - 1 - dim))
    return factor_of


def gaussian(stream_key, dims, deviation, most, pieces=(), held_as=jnp.bfloat16):
    factor_of = levels(stream_key, dims, pieces, -0.22, 0.18) if pieces else 1.0
    array = jax.random.normal(stream_key, dims, jnp.float32) * deviation * factor_of
    return jnp.minimum(jnp.maximum(array, -most), most).astype(held_as)


def setup_inputs(seed: int = 0) -> dict:
    key_list = jax.random.split(jax.random.key(seed), 8)
    features = gaussian(key_list[0], (NODES, HID), 1.0, 6.0, ((0, 32),))
    node_order = draw_node_order(jax.random.fold_in(key_list[7], 71), 0)
    layer_weight = gaussian(key_list[2], (HID, HID), HID ** -0.5, 0.375)
    layer_bias = gaussian(key_list[3], (HID,), 0.5, 3.0, (), jnp.float32)
    tile_values = jnp.clip(jnp.exp(math.log(0.049804688) - 3.9086586 * jax.random.uniform(key_list[4], (N_ROWS * N_REP * TILE_CAP, TILE, TILE), jnp.float32) ** levels(key_list[4], (N_ROWS * N_REP * TILE_CAP, TILE, TILE), ((0, 32),), -0.2, 0.2)), 0.0009994507, 0.049804688).astype(jnp.bfloat16)
    tile_coords = draw_tile_coords(jax.random.fold_in(key_list[7], 71), 0)
    tile_count = draw_tile_count(jax.random.fold_in(key_list[7], 71), 0)
    return {"features": features, "node_order": node_order, "layer_weight": layer_weight, "layer_bias": layer_bias, "tile_values": tile_values, "tile_coords": tile_coords, "tile_count": tile_count}


def aggregate(projected, tile_values, tile_coords, tile_count):
    group_total = N_ROWS * N_REP
    sources = projected.reshape(NODES // TILE, TILE, HID)
    values_grouped = tile_values.reshape(group_total, TILE_CAP, TILE, TILE)
    coords_grouped = tile_coords.reshape(group_total, TILE_CAP, 2)

    def one_group(inputs):
        values_now, coords_now, count_now, group_index = inputs
        gathered = sources[coords_now[:, 1]]
        products = jnp.einsum("tij,tjf->tif", values_now.astype(jnp.float32), gathered.astype(jnp.float32), precision=lax.Precision.HIGHEST)
        live_mask = (jnp.arange(TILE_CAP, dtype=jnp.int32) < count_now).astype(jnp.float32)
        local_rows = coords_now[:, 0] - (group_index // N_REP) * TILE_ROWS
        selector = (local_rows[None, :] == jnp.arange(TILE_ROWS, dtype=jnp.int32)[:, None]).astype(jnp.float32) * live_mask[None, :]
        summed = jnp.einsum("qt,tif->qif", selector, products, precision=lax.Precision.HIGHEST)
        return summed.reshape(ROW_DEV, HID).astype(jnp.bfloat16)

    partials = lax.map(one_group, (values_grouped, coords_grouped, tile_count, jnp.arange(group_total, dtype=jnp.int32)))
    blocks = partials.astype(jnp.float32).reshape(N_ROWS, N_REP, ROW_DEV, HID)
    return jnp.sum(blocks, axis=1).reshape(NODES, HID)


def reference(features, node_order, layer_weight, layer_bias, tile_values, tile_coords, tile_count):
    clustered = features[node_order]
    projected = jnp.dot(clustered, layer_weight, preferred_element_type=jnp.float32).astype(jnp.bfloat16)
    summed_total = aggregate(projected, tile_values, tile_coords, tile_count)
    return jax.nn.relu(summed_total + layer_bias).astype(jnp.bfloat16)
```

```python
import functools
import jax
import jax.numpy as jnp
from jax import lax
from jax.experimental import pallas as pl
from jax.experimental.pallas import tpu as pltpu
from jax.sharding import PartitionSpec as P

AXES = ("rows", "rep")
VMEM_LIMIT = 40 * 1024 * 1024


def whole(count):
    return [pl.BlockSpec(memory_space=pltpu.VMEM)] * count


def scalars():
    return pl.BlockSpec(memory_space=pltpu.SMEM)


def cost(flops, moved):
    return pl.CostEstimate(flops=flops, bytes_accessed=moved, transcendentals=0)


def prepare_kernel(mine_ref, own_ref, got_ref, own_order_ref, got_order_ref, weight_ref, out_ref):
    shard_rows = own_ref.shape[0]

    def project(rows_ref, order_ref):
        projected = jnp.dot(
            rows_ref[...], weight_ref[...], preferred_element_type=jnp.float32
        ).astype(jnp.bfloat16)
        within = lax.rem(order_ref[...], shard_rows)
        node = lax.broadcasted_iota(jnp.int32, (shard_rows, shard_rows), 0)
        chosen = (node == within).astype(jnp.float32).astype(jnp.bfloat16)
        out_ref[...] = lax.dot_general(
            chosen, projected, (((0,), (0,)), ((), ())), preferred_element_type=jnp.float32
        ).astype(jnp.bfloat16)

    @pl.when(mine_ref[0] == 1)
    def _():
        project(own_ref, own_order_ref)

    @pl.when(mine_ref[0] == 0)
    def _():
        project(got_ref, got_order_ref)


def prepare(mine, own, got, own_order, got_order, weight):
    return pl.pallas_call(
        prepare_kernel,
        out_shape=jax.ShapeDtypeStruct(own.shape, own.dtype),
        in_specs=[scalars()] + whole(5),
        out_specs=pl.BlockSpec(memory_space=pltpu.VMEM),
        compiler_params=pltpu.CompilerParams(vmem_limit_bytes=VMEM_LIMIT),
        cost_estimate=cost(4 * own.shape[0] ** 2 * own.shape[1], 3 * own.size),
        name="prepare",
    )(mine, own, got, own_order[None], got_order[None], weight)


def stage_kernel(n_pieces, has_sum, tile_rows, base_ref, table_ref, tiles_ref, *refs):
    pieces = refs[:n_pieces]
    sum_ref = refs[n_pieces] if has_sum else None
    out_ref, dense_ref = refs[-2:]
    tile = tiles_ref.shape[1]
    slots = table_ref.shape[1]
    start = 0
    spans = []
    for i, piece in enumerate(pieces):
        count = piece.shape[0] // tile
        for j in range(count):
            for p in range(tile_rows):
                entry = table_ref[p, base_ref[i] + j]
                live = jnp.where(entry >= 0, 1.0, 0.0).astype(jnp.bfloat16)
                dense_ref[p * tile : (p + 1) * tile, start + j * tile : start + (j + 1) * tile] = (
                    tiles_ref[jnp.maximum(entry, 0)] * live
                )
        spans.append((start, start + count * tile))
        start += count * tile
    strip = 2 * tile
    for top in range(0, out_ref.shape[0], strip):
        total = sum_ref[top : top + strip] if has_sum else None
        for piece, (first, last) in zip(pieces, spans):
            product = jnp.dot(
                dense_ref[top : top + strip, first:last],
                piece[...],
                preferred_element_type=jnp.float32,
            )
            total = product if total is None else total + product
        out_ref[top : top + strip] = total


def stage(pieces, bases, table, tiles, total):
    width = pieces[0].shape[1]
    tile_rows, tile = table.shape[0], tiles.shape[1]
    depth = sum(p.shape[0] for p in pieces)
    rows = tile_rows * tile
    operands = list(pieces) + ([] if total is None else [total])
    return pl.pallas_call(
        functools.partial(stage_kernel, len(pieces), total is not None, tile_rows),
        out_shape=jax.ShapeDtypeStruct((rows, width), jnp.float32),
        in_specs=[scalars(), scalars()] + whole(1 + len(operands)),
        out_specs=pl.BlockSpec(memory_space=pltpu.VMEM),
        scratch_shapes=[pltpu.VMEM((rows, depth), jnp.bfloat16)],
        compiler_params=pltpu.CompilerParams(vmem_limit_bytes=VMEM_LIMIT),
        cost_estimate=cost(2 * rows * depth * width, 2 * rows * depth + 8 * rows * width),
        name="stage",
    )(jnp.stack(bases).astype(jnp.int32), table, tiles, *operands)


def tile_table(tile_coords, tile_count, tile_rows, slots):
    replicas = lax.axis_size("rep")
    column_ids = tile_coords[:, 1]
    slot = column_ids // (tile_rows * replicas) * tile_rows + column_ids % tile_rows
    local_row = tile_coords[:, 0] - lax.axis_index("rows") * tile_rows
    entry = jnp.arange(tile_coords.shape[0], dtype=jnp.int32)
    code = jnp.where(entry < tile_count[0], local_row * slots + slot, -1)
    at = jnp.arange(tile_rows * slots, dtype=jnp.int32)
    found = jnp.max(jnp.where(code[None, :] == at[:, None], entry[None, :], -1), axis=1)
    return found.reshape(tile_rows, slots)


def device_id(row, rep, replicas):
    return row * replicas + rep


def ring_stages(own, table, tiles, tile_rows):
    replicas, row_count = lax.axis_size("rep"), lax.axis_size("rows")
    chips = row_count // replicas
    ring = list(range(0, chips, 2)) + list(range(chips - 1, 0, -2))
    place = {chip: i for i, chip in enumerate(ring)}

    def around(step):
        return [
            (
                device_id(chip * replicas + core, rep, replicas),
                device_id(ring[(place[chip] + step) % chips] * replicas + core, rep, replicas),
            )
            for chip in range(chips)
            for core in range(replicas)
            for rep in range(replicas)
        ]

    other_core = [
        (
            device_id(chip * replicas + core, rep, replicas),
            device_id(chip * replicas + 1 - core, rep, replicas),
        )
        for chip in range(chips)
        for core in range(replicas)
        for rep in range(replicas)
    ]
    up, down = around(1), around(-1)
    row = lax.axis_index("rows")
    chip, core = row // replicas, row % replicas
    here = jnp.asarray([place[c] for c in range(chips)], jnp.int32)[chip]
    order = jnp.asarray(ring, jnp.int32)
    tile = tiles.shape[1]
    half_slots = own.shape[0] // tile

    def base(offset, side, extra=0):
        return order[(here + offset) % chips] * tile_rows + side * half_slots + extra

    def both(piece):
        return piece, lax.ppermute(piece, AXES, other_core)

    def held(pieces):
        arrays, bases = [], []
        for piece, offset, extra in pieces:
            mine, theirs = both(piece)
            arrays += [mine, theirs]
            bases += [base(offset, core, extra), base(offset, 1 - core, extra)]
        return arrays, bases

    total = stage(*held([(own, 0, 0)]), table, tiles, None)
    left, right = own, own
    for step in range(1, chips // 2):
        left, right = lax.ppermute(left, AXES, up), lax.ppermute(right, AXES, down)
        total = stage(*held([(left, -step, 0), (right, step, 0)]), table, tiles, total)
    half = own.shape[0] // 2
    left, right = lax.ppermute(left[:half], AXES, up), lax.ppermute(right[half:], AXES, down)
    far = chips // 2
    return stage(*held([(left, far, 0), (right, far, half // tile)]), table, tiles, total)


def gathered_stages(own, table, tiles, tile_rows):
    panels = lax.all_gather(own, "rows", axis=0, tiled=True)
    depth = tile_rows * tiles.shape[1]
    total = None
    for section in range(panels.shape[0] // depth):
        base = jnp.int32(section * tile_rows)
        total = stage(
            [panels[section * depth : (section + 1) * depth]], [base], table, tiles, total
        )
    return total


def shards(features, node_order, layer_weight, layer_bias, tile_values, tile_coords, tile_count):
    shard_rows, width = features.shape
    replicas, row_count = lax.axis_size("rep"), lax.axis_size("rows")
    rep, row = lax.axis_index("rep"), lax.axis_index("rows")
    tile = tile_values.shape[1]
    tile_rows = shard_rows * replicas // tile
    trade = [
        (
            device_id(s * replicas + c, r, replicas),
            device_id(s * replicas + r, c, replicas),
        )
        for s in range(row_count // replicas)
        for r in range(replicas)
        for c in range(replicas)
        if r != c
    ]
    got = lax.ppermute(features, AXES, trade)
    got_order = lax.ppermute(node_order, AXES, trade)
    mine = (row % replicas == rep).astype(jnp.int32)[None]
    own = prepare(mine, features, got, node_order, got_order, layer_weight)
    slots = row_count // replicas * tile_rows
    table = tile_table(tile_coords, tile_count, tile_rows, slots)
    stages = ring_stages if replicas == 2 else gathered_stages
    total = stages(own, table, tile_values, tile_rows).astype(jnp.bfloat16)

    def part(of):
        return lax.dynamic_slice_in_dim(total, of * shard_rows, shard_rows, 0)

    result = part(rep).astype(jnp.float32)
    for step in range(1, replicas):
        result += lax.ppermute(
            part((rep + step) % replicas),
            "rep",
            [(r, (r + step) % replicas) for r in range(replicas)],
        ).astype(jnp.float32)
    return jax.nn.relu(result + layer_bias).astype(jnp.bfloat16)


def solution(mesh):
    placed = (
        P(("rows", "rep"), None),
        P(("rows", "rep")),
        P(),
        P(),
        P(("rows", "rep"), None, None),
        P(("rows", "rep"), None),
        P(("rows", "rep")),
    )
    return jax.shard_map(
        shards, mesh=mesh, in_specs=placed, out_specs=P(("rows", "rep"), None), check_vma=False
    )
```

```python
import functools
import jax
import jax.numpy as jnp
from jax import lax
from jax.experimental import pallas as pl
from jax.experimental.pallas import tpu as pltpu
from jax.sharding import PartitionSpec as P

AXES = ("rows", "rep")
MIB = 1024 * 1024
VMEM = pl.BlockSpec(memory_space=pltpu.VMEM)
ANY = pl.BlockSpec(memory_space=pl.ANY)
HBM = pl.BlockSpec(memory_space=pltpu.HBM)


def in_hbm(*arrays):
    return [pltpu.with_memory_space_constraint(a, pltpu.HBM) for a in arrays]


def cost(flops, moved):
    return pl.CostEstimate(flops=flops, bytes_accessed=moved, transcendentals=0)


def prepare_kernel(rows_hbm, order_hbm, weight_hbm, out_ref, rows, order, weight, sems):
    copies = [
        pltpu.make_async_copy(src, dst, sems.at[i])
        for i, (src, dst) in enumerate(
            ((order_hbm, order), (weight_hbm, weight), (rows_hbm, rows))
        )
    ]
    for copy in copies:
        copy.start()
    shard_rows = rows.shape[0]
    copies[0].wait()
    within = lax.rem(order[...], shard_rows)
    node = lax.broadcasted_iota(jnp.int32, (shard_rows, shard_rows), 0)
    chosen = (node == within).astype(jnp.float32).astype(jnp.bfloat16)
    copies[1].wait()
    copies[2].wait()
    projected = jnp.dot(rows[...], weight[...], preferred_element_type=jnp.float32)
    out_ref[...] = lax.dot_general(
        chosen,
        projected.astype(jnp.bfloat16),
        (((0,), (0,)), ((), ())),
        preferred_element_type=jnp.float32,
    ).astype(jnp.bfloat16)


def prepare(features, node_order, weight):
    shard_rows, width = features.shape
    order = node_order.reshape(1, shard_rows)
    return pl.pallas_call(
        prepare_kernel,
        out_shape=jax.ShapeDtypeStruct(features.shape, features.dtype),
        in_specs=[HBM] * 3,
        out_specs=VMEM,
        scratch_shapes=[
            pltpu.VMEM(features.shape, features.dtype),
            pltpu.VMEM(order.shape, jnp.int32),
            pltpu.VMEM(weight.shape, weight.dtype),
            pltpu.SemaphoreType.DMA((3,)),
        ],
        compiler_params=pltpu.CompilerParams(vmem_limit_bytes=4 * MIB),
        cost_estimate=cost(4 * shard_rows * shard_rows * width, 4 * features.size),
        name="prepare",
    )(*in_hbm(features, order, weight))


def ring_chip(place, chips):
    return 2 * place if place < chips // 2 else 2 * (chips - 1 - place) + 1


def ring_place(chip, chips):
    return jnp.where(chip % 2 == 0, chip // 2, chips - 1 - chip // 2)


class Layout:
    def __init__(self, halves, sections, replicas, tile_rows, groups, tile, slots):
        self.halves, self.sections, self.replicas = halves, sections, replicas
        self.tile_rows, self.groups, self.tile, self.slots = tile_rows, groups, tile, slots
        self.width = tile_rows // 2 if halves else tile_rows
        spans = [1] + [2] * (sections // 2 - 1) + [1] if halves else [1] * sections
        self.widths = [self.width * span for span in spans]
        self.rows = groups * tile_rows
        self.line = -(-self.rows * max(self.widths) // 128) * 128

    def block(self, stage):
        return (self.rows * self.tile, self.widths[stage] * self.tile)


def plan(layout, counts, coords, table):
    sections, width, line = layout.sections, layout.width, layout.line
    row = lax.axis_index("rows")
    core = lax.rem(row, layout.replicas)
    shape = (layout.slots, layout.slots)
    square = [lax.broadcasted_iota(jnp.int32, shape, axis) for axis in (0, 1)]
    lane = lax.broadcasted_iota(jnp.int32, (1, layout.slots), 1)
    entry = lax.broadcasted_iota(jnp.int32, (layout.slots, 1), 0)
    at = lax.broadcasted_iota(jnp.int32, (1, line), 1)
    lines = [None] * len(layout.widths)
    for g in range(layout.groups):
        block_row = row if g == 0 else row + 1 - 2 * core
        tile_row, column = coords[g, 0:1], coords[g, 1:2]
        tile_row = tile_row + (g - block_row) * layout.tile_rows
        step = column // (layout.tile_rows * layout.replicas)
        across, right = width, 0
        wanted = lane < counts[g][0]
        if layout.halves:
            ahead = ring_place(step, sections) - ring_place(row // layout.replicas, sections)
            ahead = jnp.where(ahead < 0, ahead + sections, ahead)
            step = jnp.minimum(ahead, sections - ahead)
            middle = (step > 0) & (2 * step < sections)
            across = jnp.where(middle, 2 * width, width)
            right = jnp.where(middle & (ahead == step), width, 0)
            wanted = wanted & ((column // width) % 2 == core)
        code = step * line + tile_row * across + right + column % width
        code = jnp.where(wanted, code, -1).astype(jnp.float32)
        code = jnp.sum(jnp.where(square[0] == square[1], code, 0.0), axis=1, keepdims=True)
        code = code.astype(jnp.int32)
        for i in range(len(lines)):
            found = jnp.where(code == at + i * line, entry + g * layout.slots, -1)
            found = jnp.max(found.astype(jnp.float32), axis=0, keepdims=True)
            lines[i] = found if g == 0 else jnp.maximum(lines[i], found)
    for i, found in enumerate(lines):
        table[i : i + 1] = found.astype(jnp.int32)


def fill(layout, stage, table, tiles, block, sem):
    tile, width = layout.tile, layout.widths[stage]
    strip = 32

    @pl.loop(0, block.shape[0], step=strip)
    def _(top):
        rows = pl.ds(pl.multiple_of(top, strip), strip)
        block[rows] = jnp.zeros((strip, block.shape[1]), block.dtype)

    started = jnp.int32(0)
    for g in range(layout.groups):

        def line(row, started, g=g):
            row = row + g * layout.tile_rows
            top = pl.ds(pl.multiple_of(row * tile, tile), tile)
            for c in range(width):
                entry = table[stage, row * width + c]

                @pl.when(entry >= 0)
                def _(entry=entry, c=c):
                    target = block.at[top, c * tile : (c + 1) * tile]
                    source = tiles[g].at[entry - g * layout.slots]
                    pltpu.make_async_copy(source, target, sem).start()

                started = started + (entry >= 0).astype(jnp.int32)
            return started

        started = lax.fori_loop(0, layout.tile_rows, line, started)
    return started


def finish_fill(layout, tiles, started, sem):
    size = 1
    while size <= layout.slots * layout.groups:

        @pl.when((started & size) != 0)
        def _(size=size):
            for first in range(0, size, layout.slots):
                some = tiles[0].at[pl.ds(0, min(layout.slots, size - first))]
                pltpu.make_async_copy(some, some, sem).wait()

        size *= 2


def multiply(block, pieces, total, out, first_row=0, more=None):
    strip = min(256, out.shape[0])
    for top in range(0, out.shape[0], strip):
        at = pl.ds(pl.multiple_of(first_row + top, strip), strip)
        result = total[at] if total is not None else None
        if more is not None:
            result += more[top : top + strip].astype(jnp.float32)
        column = 0
        for piece in pieces:
            product = jnp.dot(
                block[at, column : column + piece.shape[0]],
                piece[...],
                preferred_element_type=jnp.float32,
            )
            result = product if result is None else result + product
            column += piece.shape[0]
        out[top : top + strip] = result.astype(out.dtype)


def first_kernel(layout, *refs):
    groups = layout.groups
    counts, coords_hbm, tiles = (refs[i * groups : (i + 1) * groups] for i in range(3))
    piece, table, block, total, first, coords, entries, coords_sems, sems = refs[3 * groups :]
    loads = [
        pltpu.make_async_copy(coords_hbm[g], coords.at[g], coords_sems.at[g])
        for g in range(groups)
    ]
    for load in loads:
        load.start()
    for load in loads:
        load.wait()
    plan(layout, counts, coords, table)
    load = pltpu.make_async_copy(table, entries, coords_sems.at[0])
    load.start()
    load.wait()
    started = fill(layout, 0, entries, tiles, first, sems.at[0])
    more = fill(layout, 1, entries, tiles, block, sems.at[1])
    finish_fill(layout, tiles, started, sems.at[0])
    multiply(first, [piece], None, total)
    finish_fill(layout, tiles, more, sems.at[1])


def next_kernel(layout, stage, n_pieces, *refs):
    groups = layout.groups
    table, tiles = refs[0], refs[1 : 1 + groups]
    block, *pieces = refs[1 + groups : 2 + groups + n_pieces]
    total, next_block, next_total, sem = refs[2 + groups + n_pieces :]
    started = fill(layout, stage + 1, table, tiles, next_block, sem)
    multiply(block, pieces, total, next_total)
    finish_fill(layout, tiles, started, sem)


def last_kernel(n_pieces, which, has_more, block, *refs):
    pieces, total, out = refs[:n_pieces], refs[n_pieces], refs[-1]
    more = refs[n_pieces + 1] if has_more else None
    multiply(block, pieces, total, out, which() * out.shape[0], more)


SMEM = pl.BlockSpec(memory_space=pltpu.SMEM)
PARAMS = pltpu.CompilerParams(vmem_limit_bytes=16 * MIB)


def in_vmem(*arrays):
    return [pltpu.with_memory_space_constraint(a, pltpu.VMEM) for a in arrays]


def stage_cost(layout, stage, width):
    rows, depth = layout.block(stage)
    return cost(2 * rows * depth * width, 4 * rows * depth + 8 * rows * width)


def first_stage(layout, groups, piece):
    counts, coords, tiles = zip(*groups)
    n, width = layout.groups, piece.shape[1]
    coords = [c.T for c in coords]
    dtype = tiles[0].dtype
    return pl.pallas_call(
        functools.partial(first_kernel, layout),
        out_shape=[
            pltpu.VMEM((len(layout.widths), layout.line), jnp.int32),
            pltpu.VMEM(layout.block(1), dtype),
            pltpu.VMEM((layout.block(0)[0], width), jnp.float32),
        ],
        in_specs=[SMEM] * n + [ANY] * 2 * n + [VMEM],
        out_specs=[VMEM] * 3,
        scratch_shapes=[
            pltpu.VMEM(layout.block(0), dtype),
            pltpu.VMEM((n, *coords[0].shape), jnp.int32),
            pltpu.SMEM((len(layout.widths), layout.line), jnp.int32),
            pltpu.SemaphoreType.DMA((n,)),
            pltpu.SemaphoreType.DMA((2,)),
        ],
        compiler_params=PARAMS,
        cost_estimate=stage_cost(layout, 0, width),
        name="first_stage",
    )(*counts, *in_hbm(coords[0]), *coords[1:], *in_hbm(tiles[0]), *tiles[1:], *in_vmem(piece))


def next_stage(layout, stage, table, groups, block, pieces, total):
    tiles = [g[2] for g in groups]
    width = total.shape[1]
    held = in_vmem(block, *pieces, total)
    return pl.pallas_call(
        functools.partial(next_kernel, layout, stage, len(pieces)),
        out_shape=[
            pltpu.VMEM(layout.block(stage + 1), block.dtype),
            pltpu.VMEM(total.shape, total.dtype),
        ],
        in_specs=[SMEM] + [ANY] * layout.groups + [VMEM] * len(held),
        out_specs=[VMEM] * 2,
        scratch_shapes=[pltpu.SemaphoreType.DMA],
        compiler_params=PARAMS,
        cost_estimate=stage_cost(layout, stage, width),
        name="next_stage",
    )(table, *in_hbm(tiles[0]), *tiles[1:], *held)


def last_stage(block, pieces, total, part, more=None, dtype=jnp.bfloat16):
    which, rows = part
    width, depth = total.shape[1], block.shape[1]
    held = in_vmem(block, *pieces, total, *([] if more is None else [more]))
    return pl.pallas_call(
        functools.partial(last_kernel, len(pieces), which, more is not None),
        out_shape=jax.ShapeDtypeStruct((rows, width), dtype),
        in_specs=[VMEM] * len(held),
        out_specs=VMEM,
        compiler_params=PARAMS,
        cost_estimate=cost(2 * rows * depth * width, 2 * rows * depth + 8 * rows * width),
        name="last_stage",
    )(*held)


def device_id(row, rep, replicas):
    return row * replicas + rep


def core_pairs(row_count, replicas):
    return [
        (device_id(row, rep, replicas), device_id(row ^ 1, rep, replicas))
        for row in range(row_count)
        for rep in range(replicas)
    ]


def ring_stages(own, groups, layout):
    replicas, row_count = lax.axis_size("rep"), lax.axis_size("rows")
    chips = row_count // replicas
    ring = [ring_chip(i, chips) for i in range(chips)]

    def around(step):
        return [
            (
                device_id(ring[p] * replicas + c, r, replicas),
                device_id(ring[(p + step) % chips] * replicas + c, r, replicas),
            )
            for p in range(chips)
            for c in range(replicas)
            for r in range(replicas)
        ]

    up, down = around(1), around(-1)
    rows, far = own.shape[0], chips // 2
    left = right = own
    for step in range(far):
        if step == far - 1:
            left, right = left[: rows // 2], right[rows // 2 :]
        left, right = lax.ppermute(left, AXES, up), lax.ppermute(right, AXES, down)
        if step == 0:
            table, block, total = first_stage(layout, groups, own)
        else:
            block, total = next_stage(layout, step, table, groups, block, pieces, total)
        left, right, total = lax.optimization_barrier((left, right, total))
        pieces = [left, right]

    parts = block.shape[0] // rows // 2

    def finish(whose, near, more=None, dtype=jnp.bfloat16):
        def which():
            rep = lax.axis_index("rep")
            return whose * parts + (rep if near else 1 - rep)

        return last_stage(block, pieces, total, (which, rows), more, dtype)

    trade = core_pairs(row_count, replicas)
    theirs = lax.ppermute(finish(1, False), AXES, trade)
    mine = lax.ppermute(finish(1, True), AXES, trade)
    got = lax.ppermute(finish(0, False, theirs), "rep", [(0, 1), (1, 0)])
    return finish(0, True, mine, jnp.float32), got


def gathered_stages(own, groups, layout):
    panels = lax.all_gather(own, "rows", axis=0, tiled=True)
    shard_rows = own.shape[0]
    replicas, rep = lax.axis_size("rep"), lax.axis_index("rep")
    depth, last = layout.block(0)[1], layout.sections - 1
    pieces = [panels[i * depth : (i + 1) * depth] for i in range(last + 1)]
    table, block, total = first_stage(layout, groups, pieces[0])
    for i in range(1, last):
        block, total = next_stage(layout, i, table, groups, block, [pieces[i]], total)
    total = last_stage(block, [pieces[last]], total, (lambda: 0, depth), None, jnp.float32)
    total = total.astype(jnp.bfloat16)

    def part(of):
        return lax.dynamic_slice_in_dim(total, of * shard_rows, shard_rows, 0)

    kept, got = part(rep).astype(jnp.float32), 0.0
    for step in range(1, replicas):
        got += lax.ppermute(
            part((rep + step) % replicas),
            "rep",
            [(r, (r + step) % replicas) for r in range(replicas)],
        ).astype(jnp.float32)
    return kept, got


def shards(features, node_order, layer_weight, layer_bias, tile_values, tile_coords, tile_count):
    shard_rows = features.shape[0]
    replicas, row_count = lax.axis_size("rep"), lax.axis_size("rows")
    rep, row = lax.axis_index("rep"), lax.axis_index("rows")
    tile_rows = shard_rows * replicas // tile_values.shape[1]
    trade = [
        (
            device_id(s * replicas + c, r, replicas),
            device_id(s * replicas + r, c, replicas),
        )
        for s in range(row_count // replicas)
        for r in range(replicas)
        for c in range(replicas)
        if r != c
    ]
    groups = [(tile_count, tile_coords, tile_values)]
    ring = replicas == 2
    if ring:
        pairs = core_pairs(row_count, replicas)
        count, coords = (lax.ppermute(x, AXES, pairs) for x in groups[0][:2])
    own = prepare(features, node_order, layer_weight)
    if ring:
        own, tiles, count, coords = lax.optimization_barrier((own, tile_values, count, coords))
        groups.append((count, coords, lax.ppermute(tiles, AXES, pairs)))
    got = lax.ppermute(own, AXES, trade)
    own = jnp.where(row % replicas == rep, own, got)
    sections = row_count // replicas
    slots, tile = tile_values.shape[:2]
    layout = Layout(ring, sections, replicas, tile_rows, len(groups), tile, slots)
    kept, got = (ring_stages if ring else gathered_stages)(own, groups, layout)
    return jax.nn.relu(kept + got + layer_bias).astype(jnp.bfloat16)


def solution(mesh):
    placed = (
        P(("rows", "rep"), None),
        P(("rows", "rep")),
        P(),
        P(),
        P(("rows", "rep"), None, None),
        P(("rows", "rep"), None),
        P(("rows", "rep")),
    )
    return jax.shard_map(
        shards, mesh=mesh, in_specs=placed, out_specs=P(("rows", "rep"), None), check_vma=False
    )
```

```python
import functools
import jax
import jax.numpy as jnp
from jax import lax
from jax.experimental import pallas as pl
from jax.experimental.pallas import tpu as pltpu
from jax.sharding import PartitionSpec as P

AXES = ("rows", "rep")
MIB = 1024 * 1024
VMEM = pl.BlockSpec(memory_space=pltpu.VMEM)
ANY = pl.BlockSpec(memory_space=pl.ANY)
HBM = pl.BlockSpec(memory_space=pltpu.HBM)


def in_hbm(*arrays):
    return [pltpu.with_memory_space_constraint(a, pltpu.HBM) for a in arrays]


def cost(flops, moved):
    return pl.CostEstimate(flops=flops, bytes_accessed=moved, transcendentals=0)


def prepare_kernel(rows_hbm, order_hbm, weight_hbm, *refs):
    *outs, rows, order, weight, sems = refs
    copies = [
        pltpu.make_async_copy(src, dst, sems.at[i])
        for i, (src, dst) in enumerate(
            ((order_hbm, order), (weight_hbm, weight), (rows_hbm, rows))
        )
    ]
    for copy in copies:
        copy.start()
    shard_rows = rows.shape[0]
    copies[0].wait()
    within = lax.rem(order[...], shard_rows)
    node = lax.broadcasted_iota(jnp.int32, (shard_rows, shard_rows), 0)
    chosen = (node == within).astype(jnp.float32).astype(jnp.bfloat16)
    copies[1].wait()
    copies[2].wait()
    projected = jnp.dot(rows[...], weight[...], preferred_element_type=jnp.float32)
    result = lax.dot_general(
        chosen,
        projected.astype(jnp.bfloat16),
        (((0,), (0,)), ((), ())),
        preferred_element_type=jnp.float32,
    ).astype(jnp.bfloat16)
    width = result.shape[1] // len(outs)
    for i, out in enumerate(outs):
        out[...] = result[:, i * width : (i + 1) * width]


def prepare(features, node_order, weight, parts):
    shard_rows, width = features.shape
    order = node_order.reshape(1, shard_rows)
    return pl.pallas_call(
        prepare_kernel,
        out_shape=[jax.ShapeDtypeStruct((shard_rows, width // parts), features.dtype)] * parts,
        in_specs=[HBM] * 3,
        out_specs=[VMEM] * parts,
        scratch_shapes=[
            pltpu.VMEM(features.shape, features.dtype),
            pltpu.VMEM(order.shape, jnp.int32),
            pltpu.VMEM(weight.shape, weight.dtype),
            pltpu.SemaphoreType.DMA((3,)),
        ],
        compiler_params=pltpu.CompilerParams(vmem_limit_bytes=4 * MIB),
        cost_estimate=cost(4 * shard_rows * shard_rows * width, 4 * features.size),
        name="prepare",
    )(*in_hbm(features, order, weight))


def ring_chip(place, chips):
    return 2 * place if place < chips // 2 else 2 * (chips - 1 - place) + 1


def ring_place(chip, chips):
    return jnp.where(chip % 2 == 0, chip // 2, chips - 1 - chip // 2)


PLACE = 4096


class Layout:
    def __init__(self, halves, sections, replicas, tile_rows, groups, tile, slots):
        self.halves, self.sections, self.replicas = halves, sections, replicas
        self.tile_rows, self.groups, self.tile, self.slots = tile_rows, groups, tile, slots
        self.width = tile_rows // 2 if halves else tile_rows
        spans = [1] + [2] * (sections // 2 - 1) + [1] if halves else [1] * sections
        self.widths = [self.width * span for span in spans]
        self.line = -(-(slots + 1) // 128) * 128
        self.lines = groups * len(self.widths)

    def block(self, stage):
        return (self.tile_rows * self.tile, self.widths[stage] * self.tile)


def plan(layout, counts, coords, table):
    sections, width, slots, line = layout.sections, layout.width, layout.slots, layout.line
    row = lax.axis_index("rows")
    core = lax.rem(row, layout.replicas)
    before, after = (lax.broadcasted_iota(jnp.int32, (slots, slots), axis) for axis in (1, 0))
    lane = lax.broadcasted_iota(jnp.int32, (1, slots), 1)
    at = lax.broadcasted_iota(jnp.int32, (1, line), 1)

    def upright(values):
        kept = jnp.where(before == after, values.astype(jnp.float32), 0.0)
        return jnp.sum(kept, axis=1, keepdims=True)

    for g in range(layout.groups):
        block_row = row if g == 0 else row + 1 - 2 * core
        tile_row, column = coords[g, 0:1], coords[g, 1:2]
        tile_row = tile_row - block_row * layout.tile_rows
        step = column // (layout.tile_rows * layout.replicas)
        across, right = width, 0
        wanted = lane < counts[g][0]
        if layout.halves:
            ahead = ring_place(step, sections) - ring_place(row // layout.replicas, sections)
            ahead = jnp.where(ahead < 0, ahead + sections, ahead)
            step = jnp.minimum(ahead, sections - ahead)
            middle = (step > 0) & (2 * step < sections)
            across = jnp.where(middle, 2 * width, width)
            right = jnp.where(middle & (ahead == step), width, 0)
            wanted = wanted & ((column // width) % 2 == 1 - core)
        step = jnp.where(wanted, step, -1)
        packed = upright((tile_row * across + right + column % width) * PLACE + lane)
        step_up = upright(step)
        same = (step_up == step.astype(jnp.float32)) & (before < after)
        rank = jnp.sum(same.astype(jnp.float32), axis=1, keepdims=True)
        for stage in range(len(layout.widths)):
            here = step_up == stage
            found = jnp.where(here & (rank.astype(jnp.int32) == at), packed, 0.0)
            found = jnp.max(found, axis=0, keepdims=True)
            count = jnp.sum(here.astype(jnp.float32), axis=0, keepdims=True)
            found = jnp.where(at == line - 1, count, found)
            n = stage * layout.groups + g
            table[n : n + 1] = found.astype(jnp.int32)


def clear(*blocks):
    strip = 128
    for block in blocks:

        @pl.loop(0, block.shape[0], step=strip)
        def _(top, block=block):
            rows = pl.ds(pl.multiple_of(top, strip), strip)
            block[rows] = jnp.zeros((strip, block.shape[1]), block.dtype)


def fill(layout, stage, g, table, tiles, block, sem):
    tile, width = layout.tile, layout.widths[stage]
    n = stage * layout.groups + g
    count = table[n, layout.line - 1]

    @pl.loop(0, count)
    def _(i):
        packed = table[n, i]
        place = lax.shift_right_logical(packed, PLACE.bit_length() - 1)
        row = lax.shift_right_logical(place, width.bit_length() - 1)
        column = place & (width - 1)
        target = block.at[
            pl.ds(pl.multiple_of(row * tile, tile), tile),
            pl.ds(pl.multiple_of(column * tile, tile), tile),
        ]
        pltpu.make_async_copy(tiles.at[packed & (PLACE - 1)], target, sem).start()

    return count


def finish_fill(layout, tiles, started, sem):
    size = 1
    while size <= layout.slots * layout.groups:

        @pl.when((started & size) != 0)
        def _(size=size):
            for first in range(0, size, layout.slots):
                some = tiles.at[pl.ds(0, min(layout.slots, size - first))]
                pltpu.make_async_copy(some, some, sem).wait()

        size *= 2


def whole(piece):
    return jnp.concatenate([part[...] for part in piece], axis=1)


def grouped(refs, parts):
    return [refs[i : i + parts] for i in range(0, len(refs), parts)]


def multiply(blocks, pieces, total, out):
    strip = min(256, blocks[0].shape[0])
    for g, block in enumerate(blocks):
        for top in range(0, block.shape[0], strip):
            to = slice(g * block.shape[0] + top, g * block.shape[0] + top + strip)
            result = None if total is None else total[to]
            column = 0
            for piece in pieces:
                depth = piece[0].shape[0]
                product = jnp.dot(
                    block[top : top + strip, column : column + depth],
                    whole(piece),
                    preferred_element_type=jnp.float32,
                )
                result = product if result is None else result + product
                column += depth
            out[to] = result


def begin_kernel(layout, *refs):
    groups = layout.groups
    counts, coords_hbm, tiles = refs[:groups], refs[groups : 2 * groups], refs[2 * groups]
    table, block, coords, entries, coords_sems, sem, table_sem = refs[2 * groups + 1 :]
    loads = [
        pltpu.make_async_copy(coords_hbm[g], coords.at[g], coords_sems.at[g])
        for g in range(groups)
    ]
    for load in loads:
        load.start()
    clear(block)
    for load in loads:
        load.wait()
    plan(layout, counts, coords, table)
    load = pltpu.make_async_copy(table, entries, table_sem)
    load.start()
    load.wait()
    started = fill(layout, 0, 0, entries, tiles, block, sem)
    finish_fill(layout, tiles, started, sem)


def first_kernel(layout, parts, *refs):
    groups = layout.groups
    table, tiles, own, refs = refs[0], refs[1 : 1 + groups], refs[1 + groups], refs[2 + groups :]
    piece, refs = refs[:parts], refs[parts:]
    outs, scratch = refs[: 1 + 2 * groups], refs[1 + 2 * groups :]
    total, seconds, lasts = outs[0], outs[1 : 1 + groups], outs[1 + groups :]
    *firsts, entries, sems, table_sem = scratch
    load = pltpu.make_async_copy(table, entries, table_sem)
    load.start()
    clear(*firsts)
    load.wait()
    last = len(layout.widths) - 1
    started = [jnp.int32(0)] * 3
    for g in range(1, groups):
        started[0] += fill(layout, 0, g, entries, tiles[g], firsts[g - 1], sems.at[0])
    clear(*seconds, *lasts)
    for g in range(groups):
        started[1] += fill(layout, 1, g, entries, tiles[g], seconds[g], sems.at[1])
        started[2] += fill(layout, last, g, entries, tiles[g], lasts[g], sems.at[2])
    finish_fill(layout, tiles[0], started[0], sems.at[0])
    multiply([own, *firsts], [piece], None, total)
    finish_fill(layout, tiles[0], started[1], sems.at[1])
    finish_fill(layout, tiles[0], started[2], sems.at[2])


def next_kernel(layout, stage, n_pieces, parts, building, *refs):
    groups = layout.groups
    if building:
        table, tiles, refs = refs[0], refs[1 : 1 + groups], refs[1 + groups :]
    blocks, refs = refs[:groups], refs[groups:]
    pieces, refs = grouped(refs[: n_pieces * parts], parts), refs[n_pieces * parts :]
    total, next_total, *rest = refs
    if building:
        *next_blocks, entries, sem, table_sem = rest
        load = pltpu.make_async_copy(table, entries, table_sem)
        load.start()
        clear(*next_blocks)
        load.wait()
        started = jnp.int32(0)
        for g in range(groups):
            started += fill(layout, stage + 1, g, entries, tiles[g], next_blocks[g], sem)
    multiply(blocks, pieces, total, next_total)
    if building:
        finish_fill(layout, tiles[0], started, sem)


def last_kernel(n_pieces, parts, whose, which, lanes, has_more, block, *refs):
    pieces, total, out = grouped(refs[: n_pieces * parts], parts), refs[n_pieces * parts], refs[-1]
    first_row = which() * out.shape[0]
    strip = min(256, out.shape[0])
    for top in range(0, out.shape[0], strip):
        at = pl.multiple_of(first_row + top, strip)
        result = total[pl.ds(whose * block.shape[0] + at, strip), lanes]
        if has_more:
            result += refs[-2][top : top + strip].astype(jnp.float32)
        column = 0
        for piece in pieces:
            depth = piece[0].shape[0]
            result += jnp.dot(
                block[pl.ds(at, strip), column : column + depth],
                whole(piece),
                preferred_element_type=jnp.float32,
            )
            column += depth
        out[top : top + strip] = result.astype(out.dtype)


def result_kernel(kept, bias, *refs):
    *got, out = refs
    width = got[0].shape[1]
    for i, part in enumerate(got):
        lanes = slice(i * width, (i + 1) * width)
        total = kept[:, lanes] + part[...].astype(jnp.float32) + bias[:, lanes]
        out[:, lanes] = jnp.maximum(total, 0.0).astype(out.dtype)


SMEM = pl.BlockSpec(memory_space=pltpu.SMEM)
PARAMS = pltpu.CompilerParams(vmem_limit_bytes=16 * MIB)


def in_vmem(*arrays):
    return [pltpu.with_memory_space_constraint(a, pltpu.VMEM) for a in arrays]


def stage_cost(layout, stage, width):
    rows, depth = layout.block(stage)
    rows *= layout.groups
    return cost(2 * rows * depth * width, 4 * rows * depth + 8 * rows * width)


def begin(layout, groups):
    counts, coords, tiles = zip(*groups)
    n, dtype = layout.groups, tiles[0].dtype
    coords = [c.T for c in coords]
    lines = (layout.lines, layout.line)
    return pl.pallas_call(
        functools.partial(begin_kernel, layout),
        out_shape=[pltpu.VMEM(lines, jnp.int32), pltpu.VMEM(layout.block(0), dtype)],
        in_specs=[SMEM] * n + [ANY] * (n + 1),
        out_specs=[VMEM] * 2,
        scratch_shapes=[
            pltpu.VMEM((n, *coords[0].shape), jnp.int32),
            pltpu.SMEM(lines, jnp.int32),
            pltpu.SemaphoreType.DMA((n,)),
            pltpu.SemaphoreType.DMA,
            pltpu.SemaphoreType.DMA,
        ],
        compiler_params=PARAMS,
        cost_estimate=cost(0, 4 * layout.block(0)[0] * layout.block(0)[1]),
        name="begin",
    )(*counts, *in_hbm(coords[0]), *coords[1:], *in_hbm(tiles[0]))


def first_stage(layout, table, groups, own, piece):
    tiles = [g[2] for g in groups]
    n, width, dtype = layout.groups, sum(x.shape[1] for x in piece), tiles[0].dtype
    last = len(layout.widths) - 1
    rows = layout.block(0)[0] * n
    outs = pl.pallas_call(
        functools.partial(first_kernel, layout, len(piece)),
        out_shape=[pltpu.VMEM((rows, width), jnp.float32)]
        + [pltpu.VMEM(layout.block(1), dtype)] * n
        + [pltpu.VMEM(layout.block(last), dtype)] * n,
        in_specs=[VMEM] + [ANY] * n + [VMEM] * (1 + len(piece)),
        out_specs=[VMEM] * (2 * n + 1),
        scratch_shapes=[pltpu.VMEM(layout.block(0), dtype)] * (n - 1)
        + [
            pltpu.SMEM(table.shape, jnp.int32),
            pltpu.SemaphoreType.DMA((3,)),
            pltpu.SemaphoreType.DMA,
        ],
        compiler_params=PARAMS,
        cost_estimate=stage_cost(layout, 0, width),
        name="first_stage",
    )(*in_vmem(table), *in_hbm(tiles[0]), *tiles[1:], *in_vmem(own, *piece))
    return outs[0], outs[1 : n + 1], outs[n + 1 :]


def next_stage(layout, stage, table, groups, blocks, pieces, total):
    tiles = [g[2] for g in groups]
    width, n = total.shape[1], layout.groups
    building = table is not None
    parts = len(pieces[0])
    held = in_vmem(*blocks, *[x for piece in pieces for x in piece], total)
    sources = [*in_vmem(table), *in_hbm(tiles[0]), *tiles[1:]] if building else []
    outs = pl.pallas_call(
        functools.partial(next_kernel, layout, stage, len(pieces), parts, building),
        out_shape=[pltpu.VMEM(total.shape, total.dtype)]
        + ([pltpu.VMEM(layout.block(stage + 1), blocks[0].dtype)] * n if building else []),
        in_specs=([VMEM] + [ANY] * n if building else []) + [VMEM] * len(held),
        out_specs=[VMEM] * (1 + n if building else 1),
        scratch_shapes=[
            pltpu.SMEM(table.shape, jnp.int32),
            pltpu.SemaphoreType.DMA,
            pltpu.SemaphoreType.DMA,
        ]
        if building
        else [],
        compiler_params=PARAMS,
        cost_estimate=stage_cost(layout, stage, width),
        name="next_stage",
    )(*sources, *held)
    return outs[0], outs[1:]


def last_stage(block, whose, pieces, total, which, rows, first_lane, more=None, dtype=jnp.bfloat16):
    parts, depth = len(pieces[0]), block.shape[1]
    width = sum(x.shape[1] for x in pieces[0])
    lanes = slice(first_lane, first_lane + width)
    held = [block, *[x for piece in pieces for x in piece], total]
    held = in_vmem(*held, *([] if more is None else [more]))
    return pl.pallas_call(
        functools.partial(
            last_kernel, len(pieces), parts, whose, which, lanes, more is not None
        ),
        out_shape=pltpu.VMEM((rows, width), dtype),
        in_specs=[VMEM] * len(held),
        out_specs=VMEM,
        compiler_params=PARAMS,
        cost_estimate=cost(2 * rows * depth * width, 2 * rows * depth + 8 * rows * width),
        name="last_stage",
    )(*held)


def result(kept, got, bias):
    return pl.pallas_call(
        result_kernel,
        out_shape=jax.ShapeDtypeStruct(kept.shape, jnp.bfloat16),
        in_specs=[VMEM] * (2 + len(got)),
        out_specs=VMEM,
        compiler_params=PARAMS,
        cost_estimate=cost(4 * kept.size, 8 * kept.size),
        name="result",
    )(kept, bias.reshape(1, -1), *got)


def device_id(row, rep, replicas):
    return row * replicas + rep


def core_pairs(row_count, replicas):
    return [
        (device_id(row, rep, replicas), device_id(row ^ 1, rep, replicas))
        for row in range(row_count)
        for rep in range(replicas)
    ]


def ring_stages(shard, groups):
    tile_count, tile_coords, tile_values = groups
    replicas, row_count = lax.axis_size("rep"), lax.axis_size("rows")
    rows, chips = shard[0].shape[0], row_count // replicas
    ring = [ring_chip(i, chips) for i in range(chips)]

    def step_on(left, right, hops=1):
        def around(step):
            return [
                (
                    device_id(ring[p] * replicas + c, r, replicas),
                    device_id(ring[(p + step) % chips] * replicas + c, r, replicas),
                )
                for p in range(chips)
                for c in range(replicas)
                for r in range(replicas)
            ]

        return [
            lax.ppermute(left, AXES, around(hops)),
            lax.ppermute(right, AXES, around(-hops)),
        ]

    pairs = core_pairs(row_count, replicas)
    count, coords = (lax.ppermute(x, AXES, pairs) for x in (tile_count, tile_coords))
    shard, tiles, count, coords = lax.optimization_barrier((shard, tile_values, count, coords))
    groups = [(tile_count, tile_coords, tile_values), (count, coords, lax.ppermute(tiles, AXES, pairs))]
    tile_rows = rows * replicas // tile_values.shape[1]
    slots, tile = tile_values.shape[:2]
    layout = Layout(True, chips, replicas, tile_rows, len(groups), tile, slots)
    give = [
        (
            device_id(row, r, replicas),
            device_id(row ^ 1, r, replicas)
            if row % replicas == r
            else device_id(row, 1 - r, replicas),
        )
        for row in range(row_count)
        for r in range(replicas)
    ]
    own = [lax.ppermute(part, AXES, give) for part in shard]
    own, (table, first) = lax.optimization_barrier((own, begin(layout, groups)))
    far = chips // 2
    held = [None, [step_on(part, part) for part in own]]
    total, blocks, lasts = first_stage(layout, table, groups, first, own)

    def pieces(step):
        return [list(piece) for piece in zip(*held[step])]

    for step in range(2, far + 1):
        sent = [[lax.optimization_barrier((x, total))[0] for x in pair] for pair in held[-1]]
        if step == far:
            sent = [(left[: rows // 2], right[rows // 2 :]) for left, right in sent]
        held.append([step_on(*pair) for pair in sent])
        using = table if step < far else None
        total, blocks = next_stage(
            layout, step - 1, using, groups, blocks, pieces(step - 1), total
        )

    def finish(whose, near, ends, first_lane, more=None, dtype=jnp.bfloat16):
        def which():
            rep = lax.axis_index("rep")
            return rep if near else 1 - rep

        return last_stage(lasts[whose], whose, ends, total, which, rows, first_lane, more, dtype)

    other = [(0, 1), (1, 0)]
    lane, got = 0, []
    for pair in held[far]:
        ends = [[x] for x in pair]
        theirs = lax.ppermute(finish(1, False, ends, lane), AXES, pairs)
        got.append(lax.ppermute(finish(0, False, ends, lane, theirs), "rep", other))
        lane += pair[0].shape[1]
    ends = pieces(far)
    mine = lax.ppermute(finish(1, True, ends, 0), AXES, pairs)
    return finish(0, True, ends, 0, mine, jnp.float32), got


def gathered_stages(shard, groups):
    shard = shard[0]
    replicas, rep = lax.axis_size("rep"), lax.axis_index("rep")
    row_count, row = lax.axis_size("rows"), lax.axis_index("rows")
    shard_rows, sections = shard.shape[0], row_count // replicas
    trade = [
        (device_id(s * replicas + c, r, replicas), device_id(s * replicas + r, c, replicas))
        for s in range(sections)
        for r in range(replicas)
        for c in range(replicas)
        if r != c
    ]
    got = lax.ppermute(shard, AXES, trade)
    own = jnp.where(row % replicas == rep, shard, got)
    panels = lax.all_gather(own, "rows", axis=0, tiled=True)
    slots, tile = groups[2].shape[:2]
    layout = Layout(False, sections, replicas, shard_rows * replicas // tile, 1, tile, slots)
    groups = [groups]
    depth, last = layout.block(0)[1], layout.sections - 1
    pieces = [[panels[i * depth : (i + 1) * depth]] for i in range(last + 1)]
    table, first = begin(layout, groups)
    total, blocks, lasts = first_stage(layout, table, groups, first, pieces[0])
    for i in range(1, last):
        using = table if i < last - 1 else None
        total, blocks = next_stage(layout, i, using, groups, blocks, [pieces[i]], total)
    total = last_stage(
        lasts[0], 0, [pieces[last]], total, lambda: 0, depth, 0, None, jnp.float32
    )
    total = total.astype(jnp.bfloat16)

    def part(of):
        return lax.dynamic_slice_in_dim(total, of * shard_rows, shard_rows, 0)

    kept, got = part(rep).astype(jnp.float32), jnp.zeros((), jnp.float32)
    for step in range(1, replicas):
        got += lax.ppermute(
            part((rep + step) % replicas),
            "rep",
            [(r, (r + step) % replicas) for r in range(replicas)],
        ).astype(jnp.float32)
    return kept + got, [jnp.zeros(kept.shape, jnp.bfloat16)]


def shards(features, node_order, layer_weight, layer_bias, tile_values, tile_coords, tile_count):
    ring = lax.axis_size("rep") == 2
    projected = prepare(features, node_order, layer_weight, 2 if ring else 1)
    stages = ring_stages if ring else gathered_stages
    kept, got = stages(projected, (tile_count, tile_coords, tile_values))
    return result(kept, got, layer_bias)


def solution(mesh):
    placed = (
        P(("rows", "rep"), None),
        P(("rows", "rep")),
        P(),
        P(),
        P(("rows", "rep"), None, None),
        P(("rows", "rep"), None),
        P(("rows", "rep")),
    )
    return jax.shard_map(
        shards, mesh=mesh, in_specs=placed, out_specs=P(("rows", "rep"), None), check_vma=False
    )
```

```python
import functools
import jax
import jax.numpy as jnp
from jax import lax
from jax.experimental import pallas as pl
from jax.experimental.pallas import tpu as pltpu
from jax.sharding import PartitionSpec as P

AXES = ("rows", "rep")
MIB = 1024 * 1024
VMEM = pl.BlockSpec(memory_space=pltpu.VMEM)
ANY = pl.BlockSpec(memory_space=pl.ANY)
HBM = pl.BlockSpec(memory_space=pltpu.HBM)


def in_hbm(*arrays):
    return [pltpu.with_memory_space_constraint(a, pltpu.HBM) for a in arrays]


def cost(flops, moved):
    return pl.CostEstimate(flops=flops, bytes_accessed=moved, transcendentals=0)


def prepare_kernel(rows_hbm, order_hbm, weight_hbm, *refs):
    *outs, rows, order, weight, sems = refs
    copies = [
        pltpu.make_async_copy(src, dst, sems.at[i])
        for i, (src, dst) in enumerate(
            ((order_hbm, order), (weight_hbm, weight), (rows_hbm, rows))
        )
    ]
    for copy in copies:
        copy.start()
    shard_rows = rows.shape[0]
    copies[0].wait()
    within = lax.rem(order[...], shard_rows)
    node = lax.broadcasted_iota(jnp.int32, (shard_rows, shard_rows), 0)
    chosen = (node == within).astype(jnp.float32).astype(jnp.bfloat16)
    copies[1].wait()
    copies[2].wait()
    projected = jnp.dot(rows[...], weight[...], preferred_element_type=jnp.float32)
    result = lax.dot_general(
        chosen,
        projected.astype(jnp.bfloat16),
        (((0,), (0,)), ((), ())),
        preferred_element_type=jnp.float32,
    ).astype(jnp.bfloat16)
    width = result.shape[1] // len(outs)
    for i, out in enumerate(outs):
        out[...] = result[:, i * width : (i + 1) * width]


def prepare(features, node_order, weight, parts):
    shard_rows, width = features.shape
    order = node_order.reshape(1, shard_rows)
    return pl.pallas_call(
        prepare_kernel,
        out_shape=[jax.ShapeDtypeStruct((shard_rows, width // parts), features.dtype)] * parts,
        in_specs=[HBM] * 3,
        out_specs=[VMEM] * parts,
        scratch_shapes=[
            pltpu.VMEM(features.shape, features.dtype),
            pltpu.VMEM(order.shape, jnp.int32),
            pltpu.VMEM(weight.shape, weight.dtype),
            pltpu.SemaphoreType.DMA((3,)),
        ],
        compiler_params=pltpu.CompilerParams(vmem_limit_bytes=4 * MIB),
        cost_estimate=cost(4 * shard_rows * shard_rows * width, 4 * features.size),
        name="prepare",
    )(*in_hbm(features, order, weight))


def ring_chip(place, chips):
    return 2 * place if place < chips // 2 else 2 * (chips - 1 - place) + 1


def ring_place(chip, chips):
    return jnp.where(chip % 2 == 0, chip // 2, chips - 1 - chip // 2)


PLACE = 4096


class Layout:
    def __init__(self, halves, sections, replicas, tile_rows, groups, tile, slots):
        self.halves, self.sections, self.replicas = halves, sections, replicas
        self.tile_rows, self.groups, self.tile, self.slots = tile_rows, groups, tile, slots
        self.width = tile_rows // 2 if halves else tile_rows
        spans = [1] + [2] * (sections // 2 - 1) + [1] if halves else [1] * sections
        self.widths = [self.width * span for span in spans]
        self.line = -(-(slots + 1) // 128) * 128
        self.lines = groups * len(self.widths)

    def block(self, stage):
        return (self.tile_rows * self.tile, self.widths[stage] * self.tile)


def plan(layout, counts, coords, table):
    sections, width, slots, line = layout.sections, layout.width, layout.slots, layout.line
    row = lax.axis_index("rows")
    core = lax.rem(row, layout.replicas)
    before, after = (lax.broadcasted_iota(jnp.int32, (slots, slots), axis) for axis in (1, 0))
    lane = lax.broadcasted_iota(jnp.int32, (1, slots), 1)
    at = lax.broadcasted_iota(jnp.int32, (1, line), 1)

    def upright(values):
        kept = jnp.where(before == after, values.astype(jnp.float32), 0.0)
        return jnp.sum(kept, axis=1, keepdims=True)

    for g in range(layout.groups):
        block_row = row if g == 0 else row + 1 - 2 * core
        tile_row, column = coords[g][0:1], coords[g][1:2]
        tile_row = tile_row - block_row * layout.tile_rows
        step = column // (layout.tile_rows * layout.replicas)
        across, right = width, 0
        wanted = lane < counts[g][0]
        if layout.halves:
            ahead = ring_place(step, sections) - ring_place(row // layout.replicas, sections)
            ahead = jnp.where(ahead < 0, ahead + sections, ahead)
            step = jnp.minimum(ahead, sections - ahead)
            middle = (step > 0) & (2 * step < sections)
            across = jnp.where(middle, 2 * width, width)
            right = jnp.where(middle & (ahead == step), width, 0)
            wanted = wanted & ((column // width) % 2 == 1 - core)
        step = jnp.where(wanted, step, -1)
        packed = upright((tile_row * across + right + column % width) * PLACE + lane)
        step_up = upright(step)
        same = (step_up == step.astype(jnp.float32)) & (before < after)
        rank = jnp.sum(same.astype(jnp.float32), axis=1, keepdims=True)
        for stage in range(len(layout.widths)):
            here = step_up == stage
            found = jnp.where(here & (rank.astype(jnp.int32) == at), packed, 0.0)
            found = jnp.max(found, axis=0, keepdims=True)
            count = jnp.sum(here.astype(jnp.float32), axis=0, keepdims=True)
            found = jnp.where(at == line - 1, count, found)
            n = stage * layout.groups + g
            table[n : n + 1] = found.astype(jnp.int32)


def clear(*blocks):
    strip = 128
    for block in blocks:

        @pl.loop(0, block.shape[0], step=strip)
        def _(top, block=block):
            rows = pl.ds(pl.multiple_of(top, strip), strip)
            block[rows] = jnp.zeros((strip, block.shape[1]), block.dtype)


def fill(layout, stage, g, table, tiles, block, sem):
    tile, width = layout.tile, layout.widths[stage]
    n = stage * layout.groups + g
    count = table[n, layout.line - 1]

    @pl.loop(0, count)
    def _(i):
        packed = table[n, i]
        place = lax.shift_right_logical(packed, PLACE.bit_length() - 1)
        row = lax.shift_right_logical(place, width.bit_length() - 1)
        column = place & (width - 1)
        target = block.at[
            pl.ds(pl.multiple_of(row * tile, tile), tile),
            pl.ds(pl.multiple_of(column * tile, tile), tile),
        ]
        pltpu.make_async_copy(tiles.at[packed & (PLACE - 1)], target, sem).start()

    return count


def finish_fill(layout, tiles, started, sem):
    size = 1
    while size <= layout.slots * layout.groups:

        @pl.when((started & size) != 0)
        def _(size=size):
            for first in range(0, size, layout.slots):
                some = tiles.at[pl.ds(0, min(layout.slots, size - first))]
                pltpu.make_async_copy(some, some, sem).wait()

        size *= 2


def whole(piece):
    return jnp.concatenate([part[...] for part in piece], axis=1)


def grouped(refs, parts):
    return [refs[i : i + parts] for i in range(0, len(refs), parts)]


def multiply(blocks, pieces, total, out):
    strip = min(256, blocks[0].shape[0])
    for g, block in enumerate(blocks):
        for top in range(0, block.shape[0], strip):
            to = slice(g * block.shape[0] + top, g * block.shape[0] + top + strip)
            result = None if total is None else total[to]
            column = 0
            for piece in pieces:
                depth = piece[0].shape[0]
                product = jnp.dot(
                    block[top : top + strip, column : column + depth],
                    whole(piece),
                    preferred_element_type=jnp.float32,
                )
                result = product if result is None else result + product
                column += depth
            out[to] = result


def begin_kernel(layout, *refs):
    groups = layout.groups
    counts, coords, table = refs[:groups], refs[groups : 2 * groups], refs[2 * groups]
    plan(layout, counts, coords, table)


def first_kernel(layout, parts, *refs):
    groups = layout.groups
    table, tiles, refs = refs[0], refs[1 : 1 + groups], refs[1 + groups :]
    piece, refs = refs[:parts], refs[parts:]
    total, seconds, lasts = refs[0], refs[1 : 1 + groups], refs[1 + groups : 1 + 2 * groups]
    *firsts, entries, sems, table_sem = refs[1 + 2 * groups :]
    load = pltpu.make_async_copy(table, entries, table_sem)
    load.start()
    clear(*firsts)
    load.wait()
    last = len(layout.widths) - 1
    started = [jnp.int32(0)] * 3
    for g in range(groups):
        started[0] += fill(layout, 0, g, entries, tiles[g], firsts[g], sems.at[0])
    clear(*seconds, *lasts)
    for g in range(groups):
        started[1] += fill(layout, 1, g, entries, tiles[g], seconds[g], sems.at[1])
        started[2] += fill(layout, last, g, entries, tiles[g], lasts[g], sems.at[2])
    finish_fill(layout, tiles[0], started[0], sems.at[0])
    multiply(firsts, [piece], None, total)
    finish_fill(layout, tiles[0], started[1], sems.at[1])
    finish_fill(layout, tiles[0], started[2], sems.at[2])


def next_kernel(layout, stage, n_pieces, parts, building, *refs):
    groups = layout.groups
    if building:
        table, tiles, refs = refs[0], refs[1 : 1 + groups], refs[1 + groups :]
    blocks, refs = refs[:groups], refs[groups:]
    pieces, refs = grouped(refs[: n_pieces * parts], parts), refs[n_pieces * parts :]
    total, next_total, *rest = refs
    if building:
        *next_blocks, entries, sem, table_sem = rest
        load = pltpu.make_async_copy(table, entries, table_sem)
        load.start()
        clear(*next_blocks)
        load.wait()
        started = jnp.int32(0)
        for g in range(groups):
            started += fill(layout, stage + 1, g, entries, tiles[g], next_blocks[g], sem)
    multiply(blocks, pieces, total, next_total)
    if building:
        finish_fill(layout, tiles[0], started, sem)


def last_kernel(counts, parts, jobs, groups, *refs):
    blocks, refs = grouped(refs[: groups * len(counts)], groups), refs[groups * len(counts) :]
    n = sum(counts) * parts
    pieces, total, refs = grouped(refs[:n], parts), refs[n], refs[n + 1 :]
    added, outs = refs[: -len(jobs)], refs[-len(jobs) :]
    added = iter(added)
    for (whose, which, chosen, more), out in zip(jobs, outs):
        extra = next(added) if more else None
        rows = out.shape[0]
        first_row = which() * rows
        width = pieces[0][0].shape[1]
        lanes = slice(chosen[0] * width, (chosen[-1] + 1) * width)
        strip = min(256, rows)
        for top in range(0, rows, strip):
            at = pl.multiple_of(first_row + top, strip)
            result = total[pl.ds(whose * blocks[0][0].shape[0] + at, strip), lanes]
            if more:
                result += extra[top : top + strip].astype(jnp.float32)
            first = 0
            for count, stage in zip(counts, blocks):
                column = 0
                for piece in pieces[first : first + count]:
                    depth = piece[0].shape[0]
                    result += jnp.dot(
                        stage[whose][pl.ds(at, strip), column : column + depth],
                        whole([piece[part] for part in chosen]),
                        preferred_element_type=jnp.float32,
                    )
                    column += depth
                first += count
            out[top : top + strip] = result.astype(out.dtype)


def result_kernel(bias, *refs):
    n = len(refs) // 2
    kept, got, out = refs[:n], refs[n:-1], refs[-1]
    width = got[0].shape[1]
    for i in range(n):
        lanes = slice(i * width, (i + 1) * width)
        total = kept[i][...] + got[i][...].astype(jnp.float32) + bias[:, lanes]
        out[:, lanes] = jnp.maximum(total, 0.0).astype(out.dtype)


SMEM = pl.BlockSpec(memory_space=pltpu.SMEM)
PARAMS = pltpu.CompilerParams(vmem_limit_bytes=16 * MIB)


def in_vmem(*arrays):
    return [pltpu.with_memory_space_constraint(a, pltpu.VMEM) for a in arrays]


def stage_cost(layout, stage, width):
    rows, depth = layout.block(stage)
    rows *= layout.groups
    return cost(2 * rows * depth * width, 4 * rows * depth + 8 * rows * width)


def begin(layout, groups):
    counts, coords, _ = zip(*groups)
    n = layout.groups
    return pl.pallas_call(
        functools.partial(begin_kernel, layout),
        out_shape=pltpu.VMEM((layout.lines, layout.line), jnp.int32),
        in_specs=[SMEM] * n + [VMEM] * n,
        out_specs=VMEM,
        compiler_params=PARAMS,
        cost_estimate=cost(1000000, 4 * layout.lines * layout.line),
        name="begin",
    )(*counts, *[c.T for c in coords])


def first_stage(layout, table, groups, piece):
    tiles = [g[2] for g in groups]
    n, width, dtype = layout.groups, sum(x.shape[1] for x in piece), tiles[0].dtype
    last = len(layout.widths) - 1
    rows = layout.block(0)[0] * n
    outs = pl.pallas_call(
        functools.partial(first_kernel, layout, len(piece)),
        out_shape=[pltpu.VMEM((rows, width), jnp.float32)]
        + [pltpu.VMEM(layout.block(1), dtype)] * n
        + [pltpu.VMEM(layout.block(last), dtype)] * n,
        in_specs=[VMEM] + [ANY] * n + [VMEM] * len(piece),
        out_specs=[VMEM] * (2 * n + 1),
        scratch_shapes=[pltpu.VMEM(layout.block(0), dtype)] * n
        + [
            pltpu.SMEM(table.shape, jnp.int32),
            pltpu.SemaphoreType.DMA((3,)),
            pltpu.SemaphoreType.DMA,
        ],
        compiler_params=PARAMS,
        cost_estimate=stage_cost(layout, 0, width),
        name="first_stage",
    )(*in_vmem(table), *in_hbm(tiles[0]), *tiles[1:], *in_vmem(*piece))
    return outs[0], outs[1 : n + 1], outs[n + 1 :]


def next_stage(layout, stage, table, groups, blocks, pieces, total):
    tiles = [g[2] for g in groups]
    width, n = total.shape[1], layout.groups
    building = table is not None
    parts = len(pieces[0])
    held = in_vmem(*blocks, *[x for piece in pieces for x in piece], total)
    sources = [*in_vmem(table), *in_hbm(tiles[0]), *tiles[1:]] if building else []
    outs = pl.pallas_call(
        functools.partial(next_kernel, layout, stage, len(pieces), parts, building),
        out_shape=[pltpu.VMEM(total.shape, total.dtype)]
        + ([pltpu.VMEM(layout.block(stage + 1), blocks[0].dtype)] * n if building else []),
        in_specs=([VMEM] + [ANY] * n if building else []) + [VMEM] * len(held),
        out_specs=[VMEM] * (1 + n if building else 1),
        scratch_shapes=[
            pltpu.SMEM(table.shape, jnp.int32),
            pltpu.SemaphoreType.DMA,
            pltpu.SemaphoreType.DMA,
        ]
        if building
        else [],
        compiler_params=PARAMS,
        cost_estimate=stage_cost(layout, stage, width),
        name="next_stage",
    )(*sources, *held)
    return outs[0], outs[1:]


def last_stages(stages, total, rows, jobs):
    counts = [len(pieces) for _, pieces in stages]
    groups, parts = len(stages[0][0]), len(stages[0][1][0])
    width = stages[0][1][0][0].shape[1]
    depth = sum(blocks[0].shape[1] for blocks, _ in stages)
    held = [block for blocks, _ in stages for block in blocks]
    held += [x for _, pieces in stages for piece in pieces for x in piece] + [total]
    held = in_vmem(*held, *[job[3] for job in jobs if job[3] is not None])
    inner = [(whose, which, chosen, more is not None) for whose, which, chosen, more, _ in jobs]
    lanes = sum(width * len(job[2]) for job in jobs)
    return pl.pallas_call(
        functools.partial(last_kernel, counts, parts, inner, groups),
        out_shape=[pltpu.VMEM((rows, width * len(job[2])), job[4]) for job in jobs],
        in_specs=[VMEM] * len(held),
        out_specs=[VMEM] * len(jobs),
        compiler_params=PARAMS,
        cost_estimate=cost(2 * rows * depth * lanes, 2 * rows * depth + 8 * rows * lanes),
        name="last_stages",
    )(*held)


def result(kept, got, bias):
    rows, width = kept[0].shape
    width *= len(kept)
    return pl.pallas_call(
        result_kernel,
        out_shape=jax.ShapeDtypeStruct((rows, width), jnp.bfloat16),
        in_specs=[VMEM] * (1 + len(kept) + len(got)),
        out_specs=VMEM,
        compiler_params=PARAMS,
        cost_estimate=cost(4 * rows * width, 8 * rows * width),
        name="result",
    )(bias.reshape(1, -1), *kept, *got)


def device_id(row, rep, replicas):
    return row * replicas + rep


def core_pairs(row_count, replicas):
    return [
        (device_id(row, rep, replicas), device_id(row ^ 1, rep, replicas))
        for row in range(row_count)
        for rep in range(replicas)
    ]


def ring_stages(shard, groups):
    tile_count, tile_coords, tile_values = groups
    replicas, row_count = lax.axis_size("rep"), lax.axis_size("rows")
    rows, chips = shard[0].shape[0], row_count // replicas
    ring = [ring_chip(i, chips) for i in range(chips)]

    def step_on(array, way):
        hops = [
            (
                device_id(ring[p] * replicas + c, r, replicas),
                device_id(ring[(p + way) % chips] * replicas + c, r, replicas),
            )
            for p in range(chips)
            for c in range(replicas)
            for r in range(replicas)
        ]
        return lax.ppermute(array, AXES, hops)

    pairs = core_pairs(row_count, replicas)
    count, coords = (lax.ppermute(x, AXES, pairs) for x in (tile_count, tile_coords))
    shard, tiles, count, coords = lax.optimization_barrier((shard, tile_values, count, coords))
    groups = [(tile_count, tile_coords, tile_values), (count, coords, lax.ppermute(tiles, AXES, pairs))]
    tile_rows = rows * replicas // tile_values.shape[1]
    slots, tile = tile_values.shape[:2]
    layout = Layout(True, chips, replicas, tile_rows, len(groups), tile, slots)
    give = [
        (
            device_id(row, r, replicas),
            device_id(row ^ 1, r, replicas)
            if row % replicas == r
            else device_id(row, 1 - r, replicas),
        )
        for row in range(row_count)
        for r in range(replicas)
    ]
    own = [lax.ppermute(part, AXES, give) for part in shard]
    table = begin(layout, groups)
    own = [lax.optimization_barrier((part, table))[0] for part in own]
    far = chips // 2
    ways = 1, -1
    held = [None, [[step_on(part, way) for way in ways] for part in own]]
    total, blocks, lasts = first_stage(layout, table, groups, own)

    def pieces(step):
        return [list(piece) for piece in zip(*held[step])]

    for step in range(2, far + 1):
        sent, earlier = [], total
        for pair in held[-1]:
            if step == far:
                earlier = earlier, pair
            sent.append([lax.optimization_barrier((x, earlier))[0] for x in pair])
            earlier = total, pair
        if step < far:
            held.append([[step_on(x, way) for x, way in zip(pair, ways)] for pair in sent])
            total, blocks = next_stage(
                layout, step - 1, table, groups, blocks, pieces(step - 1), total
            )
        else:
            held.append([[step_on(sent[i][i], way)] for i, way in enumerate(ways)])
            total, _ = next_stage(layout, step - 1, None, groups, blocks, pieces(step - 1), total)

    def finish(parts, *jobs, after=None):
        stages = [(lasts, [[x for part in parts for x in held[far][part]]])]
        sums = total if after is None else lax.optimization_barrier((total, after))[0]
        return last_stages(stages, sums, rows, jobs)

    def near():
        return lax.axis_index("rep")

    def away():
        return 1 - lax.axis_index("rep")

    short, other = jnp.bfloat16, [(0, 1), (1, 0)]
    parts = list(range(len(own)))
    theirs, given = [], None
    for part in parts:
        (given,) = finish(parts[: part + 1], (1, away, [part], None, short), after=given)
        theirs.append(lax.ppermute(given, AXES, pairs))
    got, mine, summed = [], [], None
    for part in parts:
        jobs = [(0, away, [part], theirs[part], short)]
        if part == parts[-1]:
            jobs += [(1, near, [p], None, short) for p in parts]
        summed, *rest = finish(parts[: part + 1], *jobs, after=summed)
        got.append(lax.ppermute(summed, "rep", other))
        mine += [lax.ppermute(x, AXES, pairs) for x in rest]
    jobs = [(0, near, [part], mine[part], jnp.float32) for part in parts]
    return finish(parts, *jobs, after=got[0]), got


def gathered_stages(shard, groups):
    shard = shard[0]
    replicas, rep = lax.axis_size("rep"), lax.axis_index("rep")
    row_count, row = lax.axis_size("rows"), lax.axis_index("rows")
    shard_rows, sections = shard.shape[0], row_count // replicas
    trade = [
        (device_id(s * replicas + c, r, replicas), device_id(s * replicas + r, c, replicas))
        for s in range(sections)
        for r in range(replicas)
        for c in range(replicas)
        if r != c
    ]
    got = lax.ppermute(shard, AXES, trade)
    own = jnp.where(row % replicas == rep, shard, got)
    panels = lax.all_gather(own, "rows", axis=0, tiled=True)
    slots, tile = groups[2].shape[:2]
    layout = Layout(False, sections, replicas, shard_rows * replicas // tile, 1, tile, slots)
    groups = [groups]
    depth, last = layout.block(0)[1], layout.sections - 1
    pieces = [[panels[i * depth : (i + 1) * depth]] for i in range(last + 1)]
    table = begin(layout, groups)
    total, blocks, lasts = first_stage(layout, table, groups, pieces[0])
    for i in range(1, last):
        using = table if i < last - 1 else None
        total, blocks = next_stage(layout, i, using, groups, blocks, [pieces[i]], total)
    ending = [(lasts, [pieces[last]])]
    (total,) = last_stages(ending, total, depth, [(0, lambda: 0, [0], None, jnp.float32)])
    total = total.astype(jnp.bfloat16)

    def part(of):
        return lax.dynamic_slice_in_dim(total, of * shard_rows, shard_rows, 0)

    kept, got = part(rep).astype(jnp.float32), jnp.zeros((), jnp.float32)
    for step in range(1, replicas):
        got += lax.ppermute(
            part((rep + step) % replicas),
            "rep",
            [(r, (r + step) % replicas) for r in range(replicas)],
        ).astype(jnp.float32)
    return [kept + got], [jnp.zeros(kept.shape, jnp.bfloat16)]


def shards(features, node_order, layer_weight, layer_bias, tile_values, tile_coords, tile_count):
    ring = lax.axis_size("rep") == 2
    projected = prepare(features, node_order, layer_weight, 2 if ring else 1)
    stages = ring_stages if ring else gathered_stages
    kept, got = stages(projected, (tile_count, tile_coords, tile_values))
    return result(kept, got, layer_bias)


def solution(mesh):
    placed = (
        P(("rows", "rep"), None),
        P(("rows", "rep")),
        P(),
        P(),
        P(("rows", "rep"), None, None),
        P(("rows", "rep"), None),
        P(("rows", "rep")),
    )
    return jax.shard_map(
        shards, mesh=mesh, in_specs=placed, out_specs=P(("rows", "rep"), None), check_vma=False
    )
```

```python
import functools
import jax
import jax.numpy as jnp
from jax import lax
from jax.experimental import pallas as pl
from jax.experimental.pallas import tpu as pltpu
from jax.sharding import PartitionSpec as P

AXES = ("rows", "rep")
MIB = 1024 * 1024
VMEM = pl.BlockSpec(memory_space=pltpu.VMEM)
ANY = pl.BlockSpec(memory_space=pl.ANY)
HBM = pl.BlockSpec(memory_space=pltpu.HBM)


def in_hbm(*arrays):
    return [pltpu.with_memory_space_constraint(a, pltpu.HBM) for a in arrays]


def cost(flops, moved):
    return pl.CostEstimate(flops=flops, bytes_accessed=moved, transcendentals=0)


def prepare_kernel(rows_hbm, order_hbm, weight_hbm, *refs):
    *outs, rows, order, weight, sems = refs
    copies = [
        pltpu.make_async_copy(src, dst, sems.at[i])
        for i, (src, dst) in enumerate(
            ((order_hbm, order), (weight_hbm, weight), (rows_hbm, rows))
        )
    ]
    for copy in copies:
        copy.start()
    shard_rows = rows.shape[0]
    copies[0].wait()
    within = lax.rem(order[...], shard_rows)
    node = lax.broadcasted_iota(jnp.int32, (shard_rows, shard_rows), 0)
    chosen = (node == within).astype(jnp.float32).astype(jnp.bfloat16)
    copies[1].wait()
    copies[2].wait()
    projected = jnp.dot(rows[...], weight[...], preferred_element_type=jnp.float32)
    result = lax.dot_general(
        chosen,
        projected.astype(jnp.bfloat16),
        (((0,), (0,)), ((), ())),
        preferred_element_type=jnp.float32,
    ).astype(jnp.bfloat16)
    width = result.shape[1] // len(outs)
    for i, out in enumerate(outs):
        out[...] = result[:, i * width : (i + 1) * width]


def prepare(features, node_order, weight, parts):
    shard_rows, width = features.shape
    order = node_order.reshape(1, shard_rows)
    return pl.pallas_call(
        prepare_kernel,
        out_shape=[jax.ShapeDtypeStruct((shard_rows, width // parts), features.dtype)] * parts,
        in_specs=[HBM] * 3,
        out_specs=[VMEM] * parts,
        scratch_shapes=[
            pltpu.VMEM(features.shape, features.dtype),
            pltpu.VMEM(order.shape, jnp.int32),
            pltpu.VMEM(weight.shape, weight.dtype),
            pltpu.SemaphoreType.DMA((3,)),
        ],
        compiler_params=pltpu.CompilerParams(vmem_limit_bytes=4 * MIB),
        cost_estimate=cost(4 * shard_rows * shard_rows * width, 4 * features.size),
        name="prepare",
    )(*in_hbm(features, order, weight))


def ring_chip(place, chips):
    return 2 * place if place < chips // 2 else 2 * (chips - 1 - place) + 1


def ring_place(chip, chips):
    return jnp.where(chip % 2 == 0, chip // 2, chips - 1 - chip // 2)


PLACE = 4096


class Layout:
    def __init__(self, halves, sections, replicas, tile_rows, groups, tile, slots):
        self.halves, self.sections, self.replicas = halves, sections, replicas
        self.tile_rows, self.groups, self.tile, self.slots = tile_rows, groups, tile, slots
        self.width = tile_rows // 2 if halves else tile_rows
        spans = [1] + [2] * (sections // 2 - 1) + [1] if halves else [1] * sections
        self.widths = [self.width * span for span in spans]
        self.line = -(-(slots + 1) // 128) * 128
        self.lines = groups * len(self.widths)

    def block(self, stage):
        return (self.tile_rows * self.tile, self.widths[stage] * self.tile)


def plan(layout, counts, coords, table):
    sections, width, slots, line = layout.sections, layout.width, layout.slots, layout.line
    row = lax.axis_index("rows")
    core = lax.rem(row, layout.replicas)
    before, after = (lax.broadcasted_iota(jnp.int32, (slots, slots), axis) for axis in (1, 0))
    lane = lax.broadcasted_iota(jnp.int32, (1, slots), 1)
    at = lax.broadcasted_iota(jnp.int32, (1, line), 1)

    def upright(values):
        kept = jnp.where(before == after, values.astype(jnp.float32), 0.0)
        return jnp.sum(kept, axis=1, keepdims=True)

    for g in range(layout.groups):
        block_row = row if g == 0 else row + 1 - 2 * core
        tile_row, column = coords[g][0:1], coords[g][1:2]
        tile_row = tile_row - block_row * layout.tile_rows
        step = column // (layout.tile_rows * layout.replicas)
        across, right = width, 0
        wanted = lane < counts[g][0]
        if layout.halves:
            ahead = ring_place(step, sections) - ring_place(row // layout.replicas, sections)
            ahead = jnp.where(ahead < 0, ahead + sections, ahead)
            step = jnp.minimum(ahead, sections - ahead)
            middle = (step > 0) & (2 * step < sections)
            across = jnp.where(middle, 2 * width, width)
            right = jnp.where(middle & (ahead == step), width, 0)
            wanted = wanted & ((column // width) % 2 == 1 - core)
        step = jnp.where(wanted, step, -1)
        packed = upright((tile_row * across + right + column % width) * PLACE + lane)
        step_up = upright(step)
        same = (step_up == step.astype(jnp.float32)) & (before < after)
        rank = jnp.sum(same.astype(jnp.float32), axis=1, keepdims=True)
        for stage in range(len(layout.widths)):
            here = step_up == stage
            found = jnp.where(here & (rank.astype(jnp.int32) == at), packed, 0.0)
            found = jnp.max(found, axis=0, keepdims=True)
            count = jnp.sum(here.astype(jnp.float32), axis=0, keepdims=True)
            found = jnp.where(at == line - 1, count, found)
            n = stage * layout.groups + g
            table[n : n + 1] = found.astype(jnp.int32)


def clear(*blocks):
    strip = 128
    for block in blocks:

        @pl.loop(0, block.shape[0], step=strip)
        def _(top, block=block):
            rows = pl.ds(pl.multiple_of(top, strip), strip)
            block[rows] = jnp.zeros((strip, block.shape[1]), block.dtype)


def fill(layout, stage, g, table, tiles, block, sem):
    tile, width = layout.tile, layout.widths[stage]
    n = stage * layout.groups + g
    count = table[n, layout.line - 1]

    @pl.loop(0, count)
    def _(i):
        packed = table[n, i]
        place = lax.shift_right_logical(packed, PLACE.bit_length() - 1)
        row = lax.shift_right_logical(place, width.bit_length() - 1)
        column = place & (width - 1)
        target = block.at[
            pl.ds(pl.multiple_of(row * tile, tile), tile),
            pl.ds(pl.multiple_of(column * tile, tile), tile),
        ]
        pltpu.make_async_copy(tiles.at[packed & (PLACE - 1)], target, sem).start()

    return count


def finish_fill(layout, tiles, started, sem):
    size = 1
    while size <= layout.slots * layout.groups:

        @pl.when((started & size) != 0)
        def _(size=size):
            for first in range(0, size, layout.slots):
                some = tiles.at[pl.ds(0, min(layout.slots, size - first))]
                pltpu.make_async_copy(some, some, sem).wait()

        size *= 2


def whole(piece):
    return jnp.concatenate([part[...] for part in piece], axis=1)


def grouped(refs, parts):
    return [refs[i : i + parts] for i in range(0, len(refs), parts)]


def multiply(blocks, pieces, total, out, first_row=0):
    for g, block in enumerate(blocks):
        strip = min(256, block.shape[0])
        for top in range(0, block.shape[0], strip):
            start = first_row + g * block.shape[0] + top
            to = slice(start, start + strip)
            result = None if total is None else total[to]
            column = 0
            for piece in pieces:
                depth = piece[0].shape[0]
                product = jnp.dot(
                    block[top : top + strip, column : column + depth],
                    whole(piece),
                    preferred_element_type=jnp.float32,
                )
                result = product if result is None else result + product
                column += depth
            out[to] = result


def begin_kernel(layout, *refs):
    groups = layout.groups
    counts, coords, table = refs[:groups], refs[groups : 2 * groups], refs[2 * groups]
    plan(layout, counts, coords, table)
    clear(*refs[2 * groups + 1 :])


def first_kernel(layout, parts, *refs):
    groups = layout.groups
    table, tiles, refs = refs[0], refs[1 : 1 + groups], refs[1 + groups :]
    piece, refs = refs[:parts], refs[parts + groups :]
    total, seconds, lasts = refs[0], refs[1 : 1 + groups], refs[1 + groups : 1 + 2 * groups]
    *firsts, entries, sems, table_sem = refs[1 + 2 * groups :]
    load = pltpu.make_async_copy(table, entries, table_sem)
    load.start()
    clear(*firsts)
    load.wait()
    last = len(layout.widths) - 1
    started = [jnp.int32(0)] * 3
    for g in range(groups):
        started[0] += fill(layout, 0, g, entries, tiles[g], firsts[g], sems.at[0])
    clear(*lasts)
    for g in range(groups):
        started[1] += fill(layout, 1, g, entries, tiles[g], seconds[g], sems.at[1])
        started[2] += fill(layout, last, g, entries, tiles[g], lasts[g], sems.at[2])
    finish_fill(layout, tiles[0], started[0], sems.at[0])
    multiply(firsts, [piece], None, total)
    finish_fill(layout, tiles[0], started[1], sems.at[1])
    finish_fill(layout, tiles[0], started[2], sems.at[2])


def next_kernel(layout, stage, n_pieces, parts, building, *refs):
    groups = layout.groups
    if building:
        table, tiles, refs = refs[0], refs[1 : 1 + groups], refs[1 + groups :]
    blocks, refs = refs[:groups], refs[groups:]
    pieces, refs = grouped(refs[: n_pieces * parts], parts), refs[n_pieces * parts :]
    total, refs = refs[0], refs[1 + (groups if building else 0) :]
    next_total, *rest = refs
    if building:
        *next_blocks, entries, sem, table_sem = rest
        load = pltpu.make_async_copy(table, entries, table_sem)
        load.start()
    multiply(blocks[:1], pieces, total, next_total)
    if building:
        load.wait()
        started = jnp.int32(0)
        for g in range(groups):
            started += fill(layout, stage + 1, g, entries, tiles[g], next_blocks[g], sem)
    multiply(blocks[1:], pieces, total, next_total, blocks[0].shape[0])
    if building:
        finish_fill(layout, tiles[0], started, sem)


def last_kernel(counts, parts, jobs, groups, *refs):
    blocks, refs = grouped(refs[: groups * len(counts)], groups), refs[groups * len(counts) :]
    n = sum(counts) * parts
    pieces, total, refs = grouped(refs[:n], parts), refs[n], refs[n + 1 :]
    added, outs = refs[: -len(jobs)], refs[-len(jobs) :]
    added = iter(added)
    for (whose, which, chosen, more), out in zip(jobs, outs):
        extra = next(added) if more else None
        rows = out.shape[0]
        first_row = which() * rows
        width = pieces[0][0].shape[1]
        lanes = slice(chosen[0] * width, (chosen[-1] + 1) * width)
        strip = min(256, rows)
        for top in range(0, rows, strip):
            at = pl.multiple_of(first_row + top, strip)
            result = total[pl.ds(whose * blocks[0][0].shape[0] + at, strip), lanes]
            if more:
                result += extra[top : top + strip].astype(jnp.float32)
            first = 0
            for count, stage in zip(counts, blocks):
                column = 0
                for piece in pieces[first : first + count]:
                    depth = piece[0].shape[0]
                    result += jnp.dot(
                        stage[whose][pl.ds(at, strip), column : column + depth],
                        whole([piece[part] for part in chosen]),
                        preferred_element_type=jnp.float32,
                    )
                    column += depth
                first += count
            out[top : top + strip] = result.astype(out.dtype)


def result_kernel(bias, *refs):
    n = len(refs) // 2
    kept, got, out = refs[:n], refs[n:-1], refs[-1]
    width = got[0].shape[1]
    for i in range(n):
        lanes = slice(i * width, (i + 1) * width)
        total = kept[i][...] + got[i][...].astype(jnp.float32) + bias[:, lanes]
        out[:, lanes] = jnp.maximum(total, 0.0).astype(out.dtype)


SMEM = pl.BlockSpec(memory_space=pltpu.SMEM)
PARAMS = pltpu.CompilerParams(vmem_limit_bytes=16 * MIB)


def in_vmem(*arrays):
    return [pltpu.with_memory_space_constraint(a, pltpu.VMEM) for a in arrays]


def stage_cost(layout, stage, width):
    rows, depth = layout.block(stage)
    rows *= layout.groups
    return cost(2 * rows * depth * width, 4 * rows * depth + 8 * rows * width)


def begin(layout, groups):
    counts, coords, tiles = zip(*groups)
    n = layout.groups
    middle = range(1, len(layout.widths) - 1)
    outs = pl.pallas_call(
        functools.partial(begin_kernel, layout),
        out_shape=[pltpu.VMEM((layout.lines, layout.line), jnp.int32)]
        + [pltpu.VMEM(layout.block(i), tiles[0].dtype) for i in middle for _ in range(n)],
        in_specs=[SMEM] * n + [VMEM] * n,
        out_specs=[VMEM] * (1 + n * len(middle)),
        compiler_params=PARAMS,
        cost_estimate=cost(1000000, 4 * layout.lines * layout.line),
        name="begin",
    )(*counts, *[c.T for c in coords])
    return outs[0], [None, *grouped(outs[1:], n)]


def first_stage(layout, table, groups, piece, cleared):
    tiles = [g[2] for g in groups]
    n, width, dtype = layout.groups, sum(x.shape[1] for x in piece), tiles[0].dtype
    last = len(layout.widths) - 1
    rows = layout.block(0)[0] * n
    outs = pl.pallas_call(
        functools.partial(first_kernel, layout, len(piece)),
        out_shape=[pltpu.VMEM((rows, width), jnp.float32)]
        + [pltpu.VMEM(layout.block(1), dtype)] * n
        + [pltpu.VMEM(layout.block(last), dtype)] * n,
        in_specs=[VMEM] + [ANY] * n + [VMEM] * (len(piece) + n),
        out_specs=[VMEM] * (2 * n + 1),
        scratch_shapes=[pltpu.VMEM(layout.block(0), dtype)] * n
        + [
            pltpu.SMEM(table.shape, jnp.int32),
            pltpu.SemaphoreType.DMA((3,)),
            pltpu.SemaphoreType.DMA,
        ],
        input_output_aliases={1 + n + len(piece) + i: 1 + i for i in range(n)},
        compiler_params=PARAMS,
        cost_estimate=stage_cost(layout, 0, width),
        name="first_stage",
    )(*in_vmem(table), *in_hbm(tiles[0]), *tiles[1:], *in_vmem(*piece, *cleared))
    return outs[0], outs[1 : n + 1], outs[n + 1 :]


def next_stage(layout, stage, table, groups, blocks, pieces, total, cleared=None):
    tiles = [g[2] for g in groups]
    width, n = total.shape[1], layout.groups
    building = cleared is not None
    parts = len(pieces[0])
    held = in_vmem(*blocks, *[x for piece in pieces for x in piece], total)
    sources = [*in_vmem(table), *in_hbm(tiles[0]), *tiles[1:]] if building else []
    targets = in_vmem(*cleared) if building else []
    first = len(sources) + len(held)
    outs = pl.pallas_call(
        functools.partial(next_kernel, layout, stage, len(pieces), parts, building),
        out_shape=[pltpu.VMEM(total.shape, total.dtype)]
        + [pltpu.VMEM(x.shape, x.dtype) for x in targets],
        in_specs=([VMEM] + [ANY] * n if building else []) + [VMEM] * (len(held) + len(targets)),
        out_specs=[VMEM] * (1 + len(targets)),
        scratch_shapes=[
            pltpu.SMEM(table.shape, jnp.int32),
            pltpu.SemaphoreType.DMA,
            pltpu.SemaphoreType.DMA,
        ]
        if building
        else [],
        input_output_aliases={first + i: 1 + i for i in range(len(targets))},
        compiler_params=PARAMS,
        cost_estimate=stage_cost(layout, stage, width),
        name="next_stage",
    )(*sources, *held, *targets)
    return outs[0], outs[1:]


def last_stages(stages, total, rows, jobs):
    counts = [len(pieces) for _, pieces in stages]
    groups, parts = len(stages[0][0]), len(stages[0][1][0])
    width = stages[0][1][0][0].shape[1]
    depth = sum(blocks[0].shape[1] for blocks, _ in stages)
    held = [block for blocks, _ in stages for block in blocks]
    held += [x for _, pieces in stages for piece in pieces for x in piece] + [total]
    held = in_vmem(*held, *[job[3] for job in jobs if job[3] is not None])
    inner = [(whose, which, chosen, more is not None) for whose, which, chosen, more, _ in jobs]
    lanes = sum(width * len(job[2]) for job in jobs)
    return pl.pallas_call(
        functools.partial(last_kernel, counts, parts, inner, groups),
        out_shape=[pltpu.VMEM((rows, width * len(job[2])), job[4]) for job in jobs],
        in_specs=[VMEM] * len(held),
        out_specs=[VMEM] * len(jobs),
        compiler_params=PARAMS,
        cost_estimate=cost(2 * rows * depth * lanes, 2 * rows * depth + 8 * rows * lanes),
        name="last_stages",
    )(*held)


def result(kept, got, bias):
    rows, width = kept[0].shape
    width *= len(kept)
    return pl.pallas_call(
        result_kernel,
        out_shape=jax.ShapeDtypeStruct((rows, width), jnp.bfloat16),
        in_specs=[VMEM] * (1 + len(kept) + len(got)),
        out_specs=VMEM,
        compiler_params=PARAMS,
        cost_estimate=cost(4 * rows * width, 8 * rows * width),
        name="result",
    )(bias.reshape(1, -1), *kept, *got)


def device_id(row, rep, replicas):
    return row * replicas + rep


def core_pairs(row_count, replicas):
    return [
        (device_id(row, rep, replicas), device_id(row ^ 1, rep, replicas))
        for row in range(row_count)
        for rep in range(replicas)
    ]


def ring_stages(shard, groups):
    tile_count, tile_coords, tile_values = groups
    replicas, row_count = lax.axis_size("rep"), lax.axis_size("rows")
    rows, chips = shard[0].shape[0], row_count // replicas
    ring = [ring_chip(i, chips) for i in range(chips)]

    def step_on(array, way):
        hops = [
            (
                device_id(ring[p] * replicas + c, r, replicas),
                device_id(ring[(p + way) % chips] * replicas + c, r, replicas),
            )
            for p in range(chips)
            for c in range(replicas)
            for r in range(replicas)
        ]
        return lax.ppermute(array, AXES, hops)

    pairs = core_pairs(row_count, replicas)
    count, coords = (lax.ppermute(x, AXES, pairs) for x in (tile_count, tile_coords))
    shard, tiles, count, coords = lax.optimization_barrier((shard, tile_values, count, coords))
    groups = [(tile_count, tile_coords, tile_values), (count, coords, lax.ppermute(tiles, AXES, pairs))]
    tile_rows = rows * replicas // tile_values.shape[1]
    slots, tile = tile_values.shape[:2]
    layout = Layout(True, chips, replicas, tile_rows, len(groups), tile, slots)
    give = [
        (
            device_id(row, r, replicas),
            device_id(row ^ 1, r, replicas)
            if row % replicas == r
            else device_id(row, 1 - r, replicas),
        )
        for row in range(row_count)
        for r in range(replicas)
    ]
    own = [lax.ppermute(part, AXES, give) for part in shard]
    table, cleared = begin(layout, groups)
    own = [lax.optimization_barrier((part, table))[0] for part in own]
    far = chips // 2
    ways = 1, -1
    held = [None, [[step_on(part, way) for way in ways] for part in own]]
    total, blocks, lasts = first_stage(layout, table, groups, own, cleared[1])

    def pieces(step):
        return [list(piece) for piece in zip(*held[step])]

    for step in range(2, far + 1):
        sent, earlier = [], total
        for pair in held[-1]:
            if step == far:
                earlier = earlier, pair
            sent.append([lax.optimization_barrier((x, earlier))[0] for x in pair])
            earlier = total, pair
        if step < far:
            held.append([[step_on(x, way) for x, way in zip(pair, ways)] for pair in sent])
            total, blocks = next_stage(
                layout, step - 1, table, groups, blocks, pieces(step - 1), total, cleared[step]
            )
        else:
            held.append([[step_on(sent[i][i], way)] for i, way in enumerate(ways)])
            total, _ = next_stage(layout, step - 1, table, groups, blocks, pieces(step - 1), total)

    def finish(parts, *jobs, after=None):
        stages = [(lasts, [[x for part in parts for x in held[far][part]]])]
        sums = total if after is None else lax.optimization_barrier((total, after))[0]
        return last_stages(stages, sums, rows, jobs)

    def near():
        return lax.axis_index("rep")

    def away():
        return 1 - lax.axis_index("rep")

    short, other = jnp.bfloat16, [(0, 1), (1, 0)]
    parts = list(range(len(own)))
    theirs, given = [], None
    for part in parts:
        (given,) = finish(parts[: part + 1], (1, away, [part], None, short), after=given)
        theirs.append(lax.ppermute(given, AXES, pairs))
    got, mine, summed = [], [], None
    for part in parts:
        jobs = [(0, away, [part], theirs[part], short)]
        if part == parts[-1]:
            jobs += [(1, near, [p], None, short) for p in parts]
        summed, *rest = finish(parts[: part + 1], *jobs, after=summed)
        got.append(lax.ppermute(summed, "rep", other))
        mine += [lax.ppermute(x, AXES, pairs) for x in rest]
    jobs = [(0, near, [part], mine[part], jnp.float32) for part in parts]
    return finish(parts, *jobs, after=got[0]), got


def gathered_stages(shard, groups):
    shard = shard[0]
    replicas, rep = lax.axis_size("rep"), lax.axis_index("rep")
    row_count, row = lax.axis_size("rows"), lax.axis_index("rows")
    shard_rows, sections = shard.shape[0], row_count // replicas
    trade = [
        (device_id(s * replicas + c, r, replicas), device_id(s * replicas + r, c, replicas))
        for s in range(sections)
        for r in range(replicas)
        for c in range(replicas)
        if r != c
    ]
    got = lax.ppermute(shard, AXES, trade)
    own = jnp.where(row % replicas == rep, shard, got)
    panels = lax.all_gather(own, "rows", axis=0, tiled=True)
    slots, tile = groups[2].shape[:2]
    layout = Layout(False, sections, replicas, shard_rows * replicas // tile, 1, tile, slots)
    groups = [groups]
    depth, last = layout.block(0)[1], layout.sections - 1
    pieces = [[panels[i * depth : (i + 1) * depth]] for i in range(last + 1)]
    table, cleared = begin(layout, groups)
    total, blocks, lasts = first_stage(layout, table, groups, pieces[0], cleared[1])
    for i in range(1, last):
        using = cleared[i + 1] if i < last - 1 else None
        total, blocks = next_stage(layout, i, table, groups, blocks, [pieces[i]], total, using)
    ending = [(lasts, [pieces[last]])]
    (total,) = last_stages(ending, total, depth, [(0, lambda: 0, [0], None, jnp.float32)])
    total = total.astype(jnp.bfloat16)

    def part(of):
        return lax.dynamic_slice_in_dim(total, of * shard_rows, shard_rows, 0)

    kept, got = part(rep).astype(jnp.float32), jnp.zeros((), jnp.float32)
    for step in range(1, replicas):
        got += lax.ppermute(
            part((rep + step) % replicas),
            "rep",
            [(r, (r + step) % replicas) for r in range(replicas)],
        ).astype(jnp.float32)
    return [kept + got], [jnp.zeros(kept.shape, jnp.bfloat16)]


def shards(features, node_order, layer_weight, layer_bias, tile_values, tile_coords, tile_count):
    ring = lax.axis_size("rep") == 2
    projected = prepare(features, node_order, layer_weight, 2 if ring else 1)
    stages = ring_stages if ring else gathered_stages
    kept, got = stages(projected, (tile_count, tile_coords, tile_values))
    return result(kept, got, layer_bias)


def solution(mesh):
    placed = (
        P(("rows", "rep"), None),
        P(("rows", "rep")),
        P(),
        P(),
        P(("rows", "rep"), None, None),
        P(("rows", "rep"), None),
        P(("rows", "rep")),
    )
    return jax.shard_map(
        shards, mesh=mesh, in_specs=placed, out_specs=P(("rows", "rep"), None), check_vma=False
    )
```
